512 devices in a mesh: chan: 64 (over x, y, core), tm: 8 (over z).
Axes of the slice: x: 4, y: 8, z: 8, core: 2. Of those that a mesh axis runs over, the one named last changes fastest.
Arguments:
- spectra: bfloat16 [16384, 2048], P('chan', 'tm'), may hold values from -6 to 6
- coarse_delay: int32 [16384, 64], P('chan'), may hold values from 0 to 95, as said below
- fine_delay: int32 [64, 64, 32], P(None, 'chan'), may hold values from 0 to 31, as said below
- widths: int32 [8], replicated, may hold values from 1 to 128, as said below
Outputs:
- boxcars: bfloat16 [8, 2048, 2048], P(None, 'chan', 'tm')
The draws below stay inside these ranges and needn't reach their ends.
Inputs may be any that keep to these rules, and one draw needn't show every extreme that they name: `coarse_delay`: every entry is an integer delay; the value 95 occurs. `fine_delay`: every entry is an integer delay; the value 31 occurs. `widths`: the width 128 occurs.
All inputs are finite; a program needn't handle non-finite values.
Results may differ from the reference program's by a relative error of at most 0.0051.
Values may be sent and summed in bfloat16 or wider, within the bound.
No kernel may reach another device: no remote copies, remote signals or barrier semaphores. Data moves between devices by JAX's collectives and lax.ppermute only.
A program may use at most 64 MiB of HBM per device.

```python
import math
import jax
import jax.numpy as jnp
from jax import lax

CHANNELS = 16384
NSUB = 64
SAMPLES = 2048
NBLK = 64
DM_BLK = 32
NDM = 2048
D1MAX = 95
D2MAX = 31
WMAX = 128
NW = 8


def draw_coarse_delay(key, part):
    key = jax.random.fold_in(key, 11)
    first, second, third = jax.random.split(key, 3)
    values = jax.random.randint(first, (CHANNELS, NBLK), 0, D1MAX + 1, dtype=jnp.int32)
    row_spot = jax.random.randint(second, (), 0, CHANNELS, dtype=jnp.int32)
    col_spot = jax.random.randint(third, (), 0, NBLK, dtype=jnp.int32)
    return values.at[row_spot, col_spot].set(D1MAX)


def draw_fine_delay(key, part):
    key = jax.random.fold_in(key, 23)
    first, second, third = jax.random.split(key, 3)
    values = jax.random.randint(first, (NSUB, NBLK, DM_BLK), 0, D2MAX + 1, dtype=jnp.int32)
    sub_spot = jax.random.randint(second, (), 0, NSUB, dtype=jnp.int32)
    block_spot = jax.random.randint(third, (), 0, NBLK, dtype=jnp.int32)
    return values.at[sub_spot, block_spot, 0].set(D2MAX)


def draw_widths(key, part):
    key = jax.random.fold_in(key, 37)
    first, second = jax.random.split(key)
    values = jax.random.randint(first, (NW,), 1, WMAX + 1, dtype=jnp.int32)
    spot = jax.random.randint(second, (), 0, NW, dtype=jnp.int32)
    return values.at[spot].set(WMAX)


def block_levels(stream_key, extent, shards, least, largest):
    level = 1.0
    for position, blocks in shards:
        heights = jax.random.uniform(jax.random.fold_in(jax.random.fold_in(stream_key, 6), position), (blocks,), jnp.float32, least / len(shards), largest / len(shards))
        level = level * jnp.repeat(jnp.exp(heights), extent[position] // blocks).reshape((-1,) + (1,) * (len(extent) - 1 - position))
    return level


def bell_draw(stream_key, dims, scale, bound, shards=(), held_as=jnp.bfloat16):
    result = scale * jax.random.normal(stream_key, dims, jnp.float32)
    if shards:
        result = result * block_levels(stream_key, dims, shards, -0.22, 0.18)
    return jnp.clip(result, -bound, bound).astype(held_as)


def setup_inputs(seed: int = 0) -> dict:
    key_of = jax.random.split(jax.random.key(seed), 5)
    return {
        "spectra": bell_draw(key_of[0], (CHANNELS, SAMPLES), 1.0, 6.0, ((0, 64), (1, 8))),
        "coarse_delay": draw_coarse_delay(jax.random.fold_in(key_of[4], 71), 0),
        "fine_delay": draw_fine_delay(jax.random.fold_in(key_of[4], 71), 0),
        "widths": draw_widths(jax.random.fold_in(key_of[4], 71), 0),
    }


def reference(spectra, coarse_delay, fine_delay, widths):
    chans_per = CHANNELS // NSUB
    padded = jnp.pad(spectra.astype(jnp.float32), ((0, 0), (0, D1MAX + D2MAX)))
    span = SAMPLES + D2MAX
    offsets = jnp.arange(span, dtype=jnp.int32)

    def one_subband(index):
        rows = lax.dynamic_slice_in_dim(padded, index * chans_per, chans_per, 0)
        delays = lax.dynamic_slice_in_dim(coarse_delay, index * chans_per, chans_per, 0)

        def add_channel(total, item):
            row, delay = item
            picked = row[offsets[None, :] + delay[:, None]]
            return (total + picked, None)
        total, _ = lax.scan(add_channel, jnp.zeros((NBLK, span), jnp.float32), (rows, delays))
        return total.astype(jnp.bfloat16)
    subbands = lax.map(one_subband, jnp.arange(NSUB, dtype=jnp.int32))
    times = jnp.arange(SAMPLES, dtype=jnp.int32)

    def add_subband(total, item):
        sub, fine = item
        index = times[None, None, :] + fine[:, :, None]
        picked = jax.vmap(lambda row, where: row[where])(sub.astype(jnp.float32), index)
        return (total + picked, None)
    total, _ = lax.scan(add_subband, jnp.zeros((NBLK, DM_BLK, SAMPLES), jnp.float32), (subbands, fine_delay))
    series = total.reshape(NDM, SAMPLES) * (1.0 / math.sqrt(CHANNELS))
    extended = jnp.pad(series, ((0, 0), (0, WMAX - 1)))
    prefix = jnp.concatenate([jnp.zeros((NDM, 1), jnp.float32), jnp.cumsum(extended, axis=1)], axis=1)

    def one_width(width):
        upper = lax.dynamic_slice_in_dim(prefix, width, SAMPLES, 1)
        return ((upper - prefix[:, :SAMPLES]) / jnp.sqrt(width.astype(jnp.float32))).astype(jnp.bfloat16)
    return lax.map(one_width, widths)
```

```python
import functools
import math

import jax
import jax.numpy as jnp
from jax import lax
from jax.experimental import pallas as pl
from jax.experimental.pallas import tpu as pltpu
from jax.sharding import PartitionSpec as P

CHANNELS = 16384
D1MAX = 95
D2MAX = 31
WMAX = 128
LANES = 128
R1 = 8
Q1 = (D1MAX + 1) // R1
R2 = 4
Q2 = (D2MAX + 1) // R2
CHUNKS = 4


def shift_left(x, by):
    if by == 0:
        return x
    return jnp.concatenate([x[:, by:], jnp.zeros((x.shape[0], by), x.dtype)], axis=1)


def shift_right(x, by):
    if by == 0:
        return x
    return jnp.concatenate([jnp.zeros((x.shape[0], by), x.dtype), x[:, :-by]], axis=1)


def one_hot(delay, level):
    return jnp.where(delay == level, jnp.ones((), jnp.bfloat16), jnp.zeros((), jnp.bfloat16))


def level_sums(delay, spectra, shift, acc_ref):
    for r in range(R1):
        selector = jnp.concatenate([one_hot(delay, float(R1 * q + r)) for q in range(Q1)], axis=0)
        part = jnp.dot(selector, shift(spectra, r), preferred_element_type=jnp.float32)
        if r == 0:
            acc_ref[...] = part
        else:
            acc_ref[...] += part


def own_kernel(spectra_ref, delay_ref, out_ref, acc_ref):
    nblk, steps = out_ref.shape
    delay = delay_ref[...].astype(jnp.bfloat16)
    level_sums(delay, spectra_ref[...], shift_left, acc_ref)
    total = acc_ref[0:nblk, :]
    for q in range(1, Q1):
        total = total + shift_left(acc_ref[nblk * q : nblk * (q + 1), :], R1 * q)
    out_ref[...] = total


def next_kernel(own_ref, spectra_ref, delay_ref, out_ref, acc_ref, rows_ref):
    nblk, steps = own_ref.shape
    delay = delay_ref[...].astype(jnp.bfloat16)
    level_sums(delay, spectra_ref[...], lambda x, r: shift_right(x, R1 - r), acc_ref)
    total = jnp.zeros((nblk, steps + LANES), jnp.float32)
    for q in range(Q1):
        left = LANES - R1 * (q + 1)
        pieces = [acc_ref[nblk * q : nblk * (q + 1), :], jnp.zeros((nblk, LANES - left), jnp.float32)]
        if left:
            pieces = [jnp.zeros((nblk, left), jnp.float32)] + pieces
        total = total + jnp.concatenate(pieces, axis=1)
    rows_ref[pl.ds(0, nblk, stride=CHUNKS), :] = own_ref[:, :LANES]
    rows_ref[pl.ds(1, nblk, stride=CHUNKS), :] = own_ref[:, LANES:] + total[:, :LANES]
    rows_ref[pl.ds(2, nblk, stride=CHUNKS), :] = total[:, LANES : 2 * LANES]
    rows_ref[pl.ds(3, nblk, stride=CHUNKS), :] = total[:, 2 * LANES :]
    out_ref[...] = rows_ref[...].astype(jnp.bfloat16)


def trial_kernel(widths_ref, sub_ref, delay_ref, out_ref, rows_ref):
    trials, nsub = delay_ref.shape
    rows_ref[...] = sub_ref[...].astype(jnp.float32)
    sub = jnp.concatenate(
        [rows_ref[pl.ds(m, nsub, stride=CHUNKS), :] for m in range(CHUNKS)], axis=1
    ).astype(jnp.bfloat16)
    shifted = jnp.concatenate([shift_left(sub, r) for r in range(R2)], axis=0)
    delay = delay_ref[...]
    delay = jnp.concatenate([delay - r for r in range(R2)], axis=1).astype(jnp.bfloat16)
    selector = jnp.concatenate([one_hot(delay, float(R2 * q)) for q in range(Q2)], axis=0)
    parts = jnp.dot(selector, shifted, preferred_element_type=jnp.float32)
    series = parts[:trials]
    for q in range(1, Q2):
        series = series + shift_left(parts[trials * q : trials * (q + 1)], R2 * q)
    length = 3 * LANES
    series = series[:, :length] * (1.0 / math.sqrt(CHANNELS))
    high = series.astype(jnp.bfloat16)
    rest = series - high.astype(jnp.float32)
    middle = rest.astype(jnp.bfloat16)
    low = (rest - middle.astype(jnp.float32)).astype(jnp.bfloat16)
    before = lax.broadcasted_iota(jnp.int32, (length, length), 0)
    after = lax.broadcasted_iota(jnp.int32, (length, length), 1)
    triangle = jnp.where(before < after, 1.0, 0.0).astype(jnp.bfloat16)
    sums = jnp.dot(
        jnp.concatenate([high, middle, low], axis=0), triangle, preferred_element_type=jnp.float32
    )
    prefix = sums[:trials] + (sums[trials : 2 * trials] + sums[2 * trials :])
    columns = [prefix[:, LANES * m : LANES * (m + 1)] for m in range(3)]
    lane = lax.broadcasted_iota(jnp.int32, (trials, LANES), 1)
    for index in range(out_ref.shape[0]):
        width = widths_ref[index]
        turned = [pltpu.roll(column, LANES - width, 1) for column in columns]
        scale = 1.0 / jnp.sqrt(jnp.full((trials, LANES), width.astype(jnp.float32)))
        inside = lane < LANES - width
        for m in range(2):
            upper = jnp.where(inside, turned[m], turned[m + 1])
            out_ref[index, :, LANES * m : LANES * (m + 1)] = (
                (upper - columns[m]) * scale
            ).astype(jnp.bfloat16)


VMEM = pl.BlockSpec(memory_space=pltpu.VMEM)
SMEM = pl.BlockSpec(memory_space=pltpu.SMEM)
PARAMS = pltpu.CompilerParams(vmem_limit_bytes=16 * 1024 * 1024)


def per_device(spectra, coarse_delay, fine_delay, widths):
    channels, steps = spectra.shape
    nblk = coarse_delay.shape[1]
    nsub, _, trials = fine_delay.shape
    count = lax.axis_size("tm")
    following = lax.ppermute(spectra, "tm", [(z + 1, z) for z in range(count - 1)])
    by_block = coarse_delay.T
    sums = pltpu.VMEM((Q1 * nblk, steps), jnp.float32)
    flops = 2 * (D1MAX + 1) * nblk * channels * steps
    own = pl.pallas_call(
        own_kernel,
        out_shape=jax.ShapeDtypeStruct((nblk, steps), jnp.float32),
        in_specs=[VMEM] * 2,
        out_specs=VMEM,
        scratch_shapes=[sums],
        compiler_params=PARAMS,
        cost_estimate=pl.CostEstimate(flops=flops, bytes_accessed=1 << 20, transcendentals=0),
        name="own_sums",
    )(spectra, by_block)
    subbands = pl.pallas_call(
        next_kernel,
        out_shape=jax.ShapeDtypeStruct((nblk * CHUNKS, LANES), jnp.bfloat16),
        in_specs=[VMEM] * 3,
        out_specs=VMEM,
        scratch_shapes=[sums, pltpu.VMEM((nblk * CHUNKS, LANES), jnp.float32)],
        compiler_params=PARAMS,
        cost_estimate=pl.CostEstimate(flops=flops, bytes_accessed=1 << 20, transcendentals=0),
        name="next_sums",
    )(own, following, by_block)
    received = lax.all_to_all(subbands, "chan", split_axis=0, concat_axis=0, tiled=True)
    return pl.pallas_call(
        trial_kernel,
        out_shape=jax.ShapeDtypeStruct((widths.shape[0], trials, steps), jnp.bfloat16),
        in_specs=[SMEM, VMEM, VMEM],
        out_specs=VMEM,
        scratch_shapes=[pltpu.VMEM((nsub * CHUNKS, LANES), jnp.float32)],
        compiler_params=PARAMS,
        name="trials",
    )(widths, received, fine_delay.reshape(nsub, trials).T)


def solution(mesh):
    return jax.shard_map(
        per_device,
        mesh=mesh,
        in_specs=(P("chan", "tm"), P("chan", None), P(None, "chan", None), P()),
        out_specs=P(None, "chan", "tm"),
        check_vma=False,
    )
```

```python
import functools
import math

import jax
import jax.numpy as jnp
from jax import lax
from jax.experimental import pallas as pl
from jax.experimental.pallas import tpu as pltpu
from jax.sharding import PartitionSpec as P

CHANNELS = 16384
D1MAX = 95
D2MAX = 31
WMAX = 128
LANES = 128
R1 = 8
Q1 = (D1MAX + 1) // R1
R2 = 4
Q2 = (D2MAX + 1) // R2
CHUNKS = 4


def shift_left(x, by):
    if by == 0:
        return x
    return jnp.concatenate([x[:, by:], jnp.zeros((x.shape[0], by), x.dtype)], axis=1)


def shift_right(x, by):
    if by == 0:
        return x
    return jnp.concatenate([jnp.zeros((x.shape[0], by), x.dtype), x[:, :-by]], axis=1)


def one_hot(delay, level):
    return jnp.where(delay == level, jnp.ones((), jnp.bfloat16), jnp.zeros((), jnp.bfloat16))


def level_sums(delay, spectra, shift, acc_ref):
    for r in range(R1):
        selector = jnp.concatenate([one_hot(delay, float(R1 * q + r)) for q in range(Q1)], axis=0)
        part = jnp.dot(selector, shift(spectra, r), preferred_element_type=jnp.float32)
        if r == 0:
            acc_ref[...] = part
        else:
            acc_ref[...] += part


def own_kernel(
    spectra_hbm, delay_hbm, fine_hbm, widths_hbm,
    out_ref, selector_ref, triangle_ref, turn_ref, scale_ref,
    spectra_ref, delay_ref, fine_ref, widths_ref, acc_ref, sems,
):
    copies = [
        pltpu.make_async_copy(source, target, sems.at[i])
        for i, (source, target) in enumerate(
            [
                (spectra_hbm, spectra_ref),
                (delay_hbm, delay_ref),
                (fine_hbm, fine_ref),
                (widths_hbm, widths_ref),
            ]
        )
    ]
    for copy in copies:
        copy.start()
    length = triangle_ref.shape[0]
    before = lax.broadcasted_iota(jnp.int32, (length, length), 0)
    after = lax.broadcasted_iota(jnp.int32, (length, length), 1)
    triangle_ref[...] = jnp.where(before < after, 1.0, 0.0).astype(jnp.bfloat16)
    for copy in copies:
        copy.wait()
    nblk, steps = out_ref.shape
    delay = delay_ref[...].astype(jnp.bfloat16)
    level_sums(delay, spectra_ref[...], shift_left, acc_ref)
    total = acc_ref[0:nblk, :]
    for q in range(1, Q1):
        total = total + shift_left(acc_ref[nblk * q : nblk * (q + 1), :], R1 * q)
    out_ref[...] = total
    fine = fine_ref[...]
    fine = jnp.concatenate([fine - r for r in range(R2)], axis=1).astype(jnp.bfloat16)
    selector_ref[...] = jnp.concatenate([one_hot(fine, float(R2 * q)) for q in range(Q2)], axis=0)
    lane = lax.broadcasted_iota(jnp.int32, (1, LANES), 1)
    for index in range(turn_ref.shape[0]):
        width = jnp.full((1, LANES), widths_ref[index])
        turn_ref[index : index + 1, :] = (lane + width) & (LANES - 1)
        scale_ref[index : index + 1, :] = 1.0 / jnp.sqrt(width.astype(jnp.float32))


def next_kernel(own_ref, spectra_ref, delay_ref, out_ref, acc_ref, rows_ref):
    nblk, steps = own_ref.shape
    delay = delay_ref[...].astype(jnp.bfloat16)
    level_sums(delay, spectra_ref[...], lambda x, r: shift_right(x, R1 - r), acc_ref)
    total = jnp.zeros((nblk, steps + LANES), jnp.float32)
    for q in range(Q1):
        left = LANES - R1 * (q + 1)
        pieces = [acc_ref[nblk * q : nblk * (q + 1), :], jnp.zeros((nblk, LANES - left), jnp.float32)]
        if left:
            pieces = [jnp.zeros((nblk, left), jnp.float32)] + pieces
        total = total + jnp.concatenate(pieces, axis=1)
    rows_ref[pl.ds(0, nblk, stride=CHUNKS), :] = own_ref[:, :LANES]
    rows_ref[pl.ds(1, nblk, stride=CHUNKS), :] = own_ref[:, LANES:] + total[:, :LANES]
    rows_ref[pl.ds(2, nblk, stride=CHUNKS), :] = total[:, LANES : 2 * LANES]
    rows_ref[pl.ds(3, nblk, stride=CHUNKS), :] = total[:, 2 * LANES :]
    out_ref[...] = rows_ref[...].astype(jnp.bfloat16)


def trial_kernel(sub_ref, selector_ref, triangle_ref, turn_ref, scale_ref, out_ref, rows_ref):
    trials = out_ref.shape[1]
    nsub = sub_ref.shape[0] // CHUNKS
    rows_ref[...] = sub_ref[...].astype(jnp.float32)
    sub = jnp.concatenate(
        [rows_ref[pl.ds(m, nsub, stride=CHUNKS), :] for m in range(CHUNKS)], axis=1
    ).astype(jnp.bfloat16)
    shifted = jnp.concatenate([shift_left(sub, r) for r in range(R2)], axis=0)
    parts = jnp.dot(selector_ref[...], shifted, preferred_element_type=jnp.float32)
    series = parts[:trials]
    for q in range(1, Q2):
        series = series + shift_left(parts[trials * q : trials * (q + 1)], R2 * q)
    series = series[:, : triangle_ref.shape[0]] * (1.0 / math.sqrt(CHANNELS))
    high = series.astype(jnp.bfloat16)
    rest = series - high.astype(jnp.float32)
    middle = rest.astype(jnp.bfloat16)
    low = (rest - middle.astype(jnp.float32)).astype(jnp.bfloat16)
    sums = jnp.dot(
        jnp.concatenate([high, middle, low], axis=0),
        triangle_ref[...],
        preferred_element_type=jnp.float32,
    )
    prefix = sums[:trials] + (sums[trials : 2 * trials] + sums[2 * trials :])
    columns = [prefix[:, LANES * m : LANES * (m + 1)] for m in range(3)]
    lane = lax.broadcasted_iota(jnp.int32, (trials, LANES), 1)
    for index in range(out_ref.shape[0]):
        turn = jnp.broadcast_to(turn_ref[index : index + 1, :], (trials, LANES))
        scale = jnp.broadcast_to(scale_ref[index : index + 1, :], (trials, LANES))
        turned = [jnp.take_along_axis(column, turn, axis=1) for column in columns]
        inside = turn > lane
        for m in range(2):
            upper = jnp.where(inside, turned[m], turned[m + 1])
            out_ref[index, :, LANES * m : LANES * (m + 1)] = (
                (upper - columns[m]) * scale
            ).astype(jnp.bfloat16)


VMEM = pl.BlockSpec(memory_space=pltpu.VMEM)
ANY = pl.BlockSpec(memory_space=pl.ANY)
PARAMS = pltpu.CompilerParams(vmem_limit_bytes=16 * 1024 * 1024)


def per_device(spectra, coarse_delay, fine_delay, widths):
    channels, steps = spectra.shape
    nblk = coarse_delay.shape[1]
    nsub, _, trials = fine_delay.shape
    blocks = lax.axis_size("tm")
    following = lax.ppermute(spectra, "tm", [(z + 1, z) for z in range(blocks - 1)])
    by_block = coarse_delay.T
    sums = pltpu.VMEM((Q1 * nblk, steps), jnp.float32)
    flops = 2 * (D1MAX + 1) * nblk * channels * steps
    fine = fine_delay.reshape(nsub, trials).T
    count = widths.shape[0]
    length = steps + WMAX
    own, selector, triangle, turn, scale = pl.pallas_call(
        own_kernel,
        out_shape=[
            jax.ShapeDtypeStruct((nblk, steps), jnp.float32),
            jax.ShapeDtypeStruct((Q2 * trials, R2 * nsub), jnp.bfloat16),
            jax.ShapeDtypeStruct((length, length), jnp.bfloat16),
            jax.ShapeDtypeStruct((count, LANES), jnp.int32),
            jax.ShapeDtypeStruct((count, LANES), jnp.float32),
        ],
        in_specs=[ANY] * 4,
        out_specs=[VMEM] * 5,
        scratch_shapes=[
            pltpu.VMEM(spectra.shape, spectra.dtype),
            pltpu.VMEM(by_block.shape, by_block.dtype),
            pltpu.VMEM(fine.shape, fine.dtype),
            pltpu.SMEM(widths.shape, widths.dtype),
            sums,
            pltpu.SemaphoreType.DMA((4,)),
        ],
        compiler_params=PARAMS,
        cost_estimate=pl.CostEstimate(flops=flops, bytes_accessed=1 << 20, transcendentals=0),
        name="own_sums",
    )(spectra, by_block, fine, widths)
    subbands = pl.pallas_call(
        next_kernel,
        out_shape=jax.ShapeDtypeStruct((nblk * CHUNKS, LANES), jnp.bfloat16),
        in_specs=[VMEM] * 3,
        out_specs=VMEM,
        scratch_shapes=[sums, pltpu.VMEM((nblk * CHUNKS, LANES), jnp.float32)],
        compiler_params=PARAMS,
        cost_estimate=pl.CostEstimate(flops=flops, bytes_accessed=1 << 20, transcendentals=0),
        name="next_sums",
    )(own, following, by_block)
    received = lax.all_to_all(subbands, "chan", split_axis=0, concat_axis=0, tiled=True)
    return pl.pallas_call(
        trial_kernel,
        out_shape=jax.ShapeDtypeStruct((count, trials, steps), jnp.bfloat16),
        in_specs=[VMEM] * 5,
        out_specs=VMEM,
        scratch_shapes=[pltpu.VMEM((nsub * CHUNKS, LANES), jnp.float32)],
        compiler_params=PARAMS,
        name="trials",
    )(received, selector, triangle, turn, scale)


def solution(mesh):
    return jax.shard_map(
        per_device,
        mesh=mesh,
        in_specs=(P("chan", "tm"), P("chan", None), P(None, "chan", None), P()),
        out_specs=P(None, "chan", "tm"),
        check_vma=False,
    )
```

```python
import functools
import math

import jax
import jax.numpy as jnp
from jax import lax
from jax.experimental import pallas as pl
from jax.experimental.pallas import tpu as pltpu
from jax.sharding import PartitionSpec as P

CHANNELS = 16384
D1MAX = 95
D2MAX = 31
WMAX = 128
LANES = 128
MARGIN = D1MAX + 1
R1 = 8
Q1 = (D1MAX + 1) // R1
R2 = 4
Q2 = (D2MAX + 1) // R2
CHUNKS = 4


def shift_left(x, by):
    if by == 0:
        return x
    return jnp.concatenate([x[:, by:], jnp.zeros((x.shape[0], by), x.dtype)], axis=1)


def turn_left(x, by):
    if by == 0:
        return x
    return jnp.concatenate([x[:, by:], x[:, :by]], axis=1)


def one_hot(delay, level):
    return jnp.where(delay == level, jnp.ones((), jnp.bfloat16), jnp.zeros((), jnp.bfloat16))


def own_kernel(
    spectra_hbm, delay_hbm, out_ref, sent_ref,
    spectra_ref, delay_ref, acc_ref, before_ref, sems,
):
    copies = [
        pltpu.make_async_copy(spectra_hbm, spectra_ref, sems.at[0]),
        pltpu.make_async_copy(delay_hbm, delay_ref, sems.at[1]),
    ]
    for copy in copies:
        copy.start()
    for copy in copies:
        copy.wait()
    nblk, steps = out_ref.shape
    last = steps - LANES
    spectra = spectra_ref[...]
    delay = delay_ref[...].astype(jnp.bfloat16)
    lane = lax.broadcasted_iota(jnp.int32, (1, LANES), 1)
    for r in range(R1):
        selector = jnp.concatenate([one_hot(delay, float(R1 * q + r)) for q in range(Q1)], axis=0)
        part = jnp.dot(selector, turn_left(spectra, r), preferred_element_type=jnp.float32)
        if r == 0:
            acc_ref[...] = part
            before_ref[...] = jnp.zeros(before_ref.shape, jnp.float32)
        else:
            acc_ref[:, :last] += part[:, :last]
            over = lane >= LANES - r
            acc_ref[:, last:] += jnp.where(over, 0.0, part[:, last:])
            before_ref[...] += jnp.where(over, part[:, last:], 0.0)
    total = jnp.zeros((nblk, LANES + steps), jnp.float32)
    for q in range(Q1):
        rows = slice(nblk * q, nblk * (q + 1))
        total = total + shift_left(
            jnp.concatenate([before_ref[rows, :], acc_ref[rows, :]], axis=1), R1 * q
        )
    out_ref[...] = total[:, LANES:]
    sent_ref[...] = total[:, LANES - MARGIN : LANES - MARGIN + steps]


def ready_kernel(fine_hbm, widths_hbm, selector_ref, triangle_ref, turn_ref, scale_ref, fine_ref, widths_ref, sems):
    copies = [
        pltpu.make_async_copy(fine_hbm, fine_ref, sems.at[0]),
        pltpu.make_async_copy(widths_hbm, widths_ref, sems.at[1]),
    ]
    for copy in copies:
        copy.start()
    length = triangle_ref.shape[0]
    before = lax.broadcasted_iota(jnp.int32, (length, length), 0)
    after = lax.broadcasted_iota(jnp.int32, (length, length), 1)
    triangle_ref[...] = jnp.where(before < after, 1.0, 0.0).astype(jnp.bfloat16)
    for copy in copies:
        copy.wait()
    fine = fine_ref[...]
    fine = jnp.concatenate([fine - r for r in range(R2)], axis=1).astype(jnp.bfloat16)
    selector_ref[...] = jnp.concatenate([one_hot(fine, float(R2 * q)) for q in range(Q2)], axis=0)
    lane = lax.broadcasted_iota(jnp.int32, (1, LANES), 1)
    for index in range(turn_ref.shape[0]):
        width = jnp.full((1, LANES), widths_ref[index])
        turn_ref[index : index + 1, :] = (lane + width) & (LANES - 1)
        scale_ref[index : index + 1, :] = 1.0 / jnp.sqrt(width.astype(jnp.float32))


def join_kernel(own_ref, next_ref, out_ref, rows_ref):
    nblk, steps = own_ref.shape
    left = steps - MARGIN - LANES
    total = jnp.concatenate(
        [
            jnp.zeros((nblk, left), jnp.float32),
            next_ref[...],
            jnp.zeros((nblk, 3 * LANES - left - steps), jnp.float32),
        ],
        axis=1,
    )
    rows_ref[pl.ds(0, nblk, stride=CHUNKS), :] = own_ref[:, :LANES]
    rows_ref[pl.ds(1, nblk, stride=CHUNKS), :] = own_ref[:, LANES:] + total[:, :LANES]
    rows_ref[pl.ds(2, nblk, stride=CHUNKS), :] = total[:, LANES : 2 * LANES]
    rows_ref[pl.ds(3, nblk, stride=CHUNKS), :] = total[:, 2 * LANES :]
    out_ref[...] = rows_ref[...].astype(jnp.bfloat16)


def trial_kernel(sub_ref, selector_ref, triangle_ref, turn_ref, scale_ref, out_ref, rows_ref):
    trials = out_ref.shape[1]
    nsub = sub_ref.shape[0] // CHUNKS
    rows_ref[...] = sub_ref[...].astype(jnp.float32)
    sub = jnp.concatenate(
        [rows_ref[pl.ds(m, nsub, stride=CHUNKS), :] for m in range(CHUNKS)], axis=1
    ).astype(jnp.bfloat16)
    shifted = jnp.concatenate([shift_left(sub, r) for r in range(R2)], axis=0)
    parts = jnp.dot(selector_ref[...], shifted, preferred_element_type=jnp.float32)
    series = parts[:trials]
    for q in range(1, Q2):
        series = series + shift_left(parts[trials * q : trials * (q + 1)], R2 * q)
    series = series[:, : triangle_ref.shape[0]] * (1.0 / math.sqrt(CHANNELS))
    high = series.astype(jnp.bfloat16)
    rest = series - high.astype(jnp.float32)
    middle = rest.astype(jnp.bfloat16)
    low = (rest - middle.astype(jnp.float32)).astype(jnp.bfloat16)
    sums = jnp.dot(
        jnp.concatenate([high, middle, low], axis=0),
        triangle_ref[...],
        preferred_element_type=jnp.float32,
    )
    prefix = sums[:trials] + (sums[trials : 2 * trials] + sums[2 * trials :])
    columns = [prefix[:, LANES * m : LANES * (m + 1)] for m in range(3)]
    lane = lax.broadcasted_iota(jnp.int32, (trials, LANES), 1)
    for index in range(out_ref.shape[0]):
        turn = jnp.broadcast_to(turn_ref[index : index + 1, :], (trials, LANES))
        scale = jnp.broadcast_to(scale_ref[index : index + 1, :], (trials, LANES))
        turned = [jnp.take_along_axis(column, turn, axis=1) for column in columns]
        inside = turn > lane
        for m in range(2):
            upper = jnp.where(inside, turned[m], turned[m + 1])
            out_ref[index, :, LANES * m : LANES * (m + 1)] = (
                (upper - columns[m]) * scale
            ).astype(jnp.bfloat16)


VMEM = pl.BlockSpec(memory_space=pltpu.VMEM)
HBM = pl.BlockSpec(memory_space=pltpu.HBM)
PARAMS = pltpu.CompilerParams(vmem_limit_bytes=16 * 1024 * 1024)


def per_device(spectra, coarse_delay, fine_delay, widths):
    channels, steps = spectra.shape
    nblk = coarse_delay.shape[1]
    nsub, _, trials = fine_delay.shape
    count = widths.shape[0]
    length = steps + WMAX
    by_block = coarse_delay.T
    fine = fine_delay.reshape(nsub, trials).T
    own, sent = pl.pallas_call(
        own_kernel,
        out_shape=[jax.ShapeDtypeStruct((nblk, steps), jnp.float32)] * 2,
        in_specs=[HBM] * 2,
        out_specs=[VMEM] * 2,
        scratch_shapes=[
            pltpu.VMEM(spectra.shape, spectra.dtype),
            pltpu.VMEM(by_block.shape, by_block.dtype),
            pltpu.VMEM((Q1 * nblk, steps), jnp.float32),
            pltpu.VMEM((Q1 * nblk, LANES), jnp.float32),
            pltpu.SemaphoreType.DMA((2,)),
        ],
        compiler_params=PARAMS,
        name="own_sums",
    )(*(pltpu.with_memory_space_constraint(x, pltpu.HBM) for x in (spectra, by_block)))
    blocks = lax.axis_size("tm")
    following = lax.ppermute(sent, "tm", [(z + 1, z) for z in range(blocks - 1)])
    selector, triangle, turn, scale = pl.pallas_call(
        ready_kernel,
        out_shape=[
            jax.ShapeDtypeStruct((Q2 * trials, R2 * nsub), jnp.bfloat16),
            jax.ShapeDtypeStruct((length, length), jnp.bfloat16),
            jax.ShapeDtypeStruct((count, LANES), jnp.int32),
            jax.ShapeDtypeStruct((count, LANES), jnp.float32),
        ],
        in_specs=[HBM] * 2,
        out_specs=[VMEM] * 4,
        scratch_shapes=[
            pltpu.VMEM(fine.shape, fine.dtype),
            pltpu.SMEM(widths.shape, widths.dtype),
            pltpu.SemaphoreType.DMA((2,)),
        ],
        compiler_params=PARAMS,
        cost_estimate=pl.CostEstimate(flops=1 << 30, bytes_accessed=1 << 20, transcendentals=0),
        name="ready",
    )(*(pltpu.with_memory_space_constraint(x, pltpu.HBM) for x in (fine, widths)))
    subbands = pl.pallas_call(
        join_kernel,
        out_shape=jax.ShapeDtypeStruct((nblk * CHUNKS, LANES), jnp.bfloat16),
        in_specs=[VMEM] * 2,
        out_specs=VMEM,
        scratch_shapes=[pltpu.VMEM((nblk * CHUNKS, LANES), jnp.float32)],
        compiler_params=PARAMS,
        name="join",
    )(own, following)
    received = lax.all_to_all(subbands, "chan", split_axis=0, concat_axis=0, tiled=True)
    return pl.pallas_call(
        trial_kernel,
        out_shape=jax.ShapeDtypeStruct((count, trials, steps), jnp.bfloat16),
        in_specs=[VMEM] * 5,
        out_specs=VMEM,
        scratch_shapes=[pltpu.VMEM((nsub * CHUNKS, LANES), jnp.float32)],
        compiler_params=PARAMS,
        name="trials",
    )(received, selector, triangle, turn, scale)


def solution(mesh):
    return jax.shard_map(
        per_device,
        mesh=mesh,
        in_specs=(P("chan", "tm"), P("chan", None), P(None, "chan", None), P()),
        out_specs=P(None, "chan", "tm"),
        check_vma=False,
    )
```

```python
import functools
import math

import jax
import jax.numpy as jnp
from jax import lax
from jax.experimental import pallas as pl
from jax.experimental.pallas import tpu as pltpu
from jax.sharding import PartitionSpec as P

CHANNELS = 16384
D1MAX = 95
D2MAX = 31
WMAX = 128
LANES = 128
MARGIN = D1MAX + 1
R1 = 8
Q1 = (D1MAX + 1) // R1
R2 = 4
Q2 = (D2MAX + 1) // R2
ROOT = 41
CHUNKS = 4


def shift_left(x, by):
    if by == 0:
        return x
    return jnp.concatenate([x[:, by:], jnp.zeros((x.shape[0], by), x.dtype)], axis=1)


def turn_left(x, by):
    if by == 0:
        return x
    return jnp.concatenate([x[:, by:], x[:, :by]], axis=1)


def from_root(x, axis):
    first, second = jnp.split(x, [ROOT], axis=axis)
    return jnp.concatenate([second, first], axis=axis)


def one_hot(delay, level):
    return jnp.where(delay == level, jnp.ones((), jnp.bfloat16), jnp.zeros((), jnp.bfloat16))


def own_sums(
    spectra_hbm, delay_hbm, out_ref, sent_ref,
    spectra_ref, delay_ref, acc_ref, before_ref, sems,
):
    copies = [
        pltpu.make_async_copy(spectra_hbm, spectra_ref, sems.at[0]),
        pltpu.make_async_copy(delay_hbm, delay_ref, sems.at[1]),
    ]
    for copy in copies:
        copy.start()
    for copy in copies:
        copy.wait()
    nblk, steps = out_ref.shape
    last = steps - LANES
    spectra = spectra_ref[...]
    delay = from_root(delay_ref[...], 0).astype(jnp.bfloat16)
    lane = lax.broadcasted_iota(jnp.int32, (1, LANES), 1)
    for r in range(R1):
        selector = jnp.concatenate([one_hot(delay, float(R1 * q + r)) for q in range(Q1)], axis=0)
        part = jnp.dot(selector, turn_left(spectra, r), preferred_element_type=jnp.float32)
        if r == 0:
            acc_ref[...] = part
            before_ref[...] = jnp.zeros(before_ref.shape, jnp.float32)
        else:
            acc_ref[:, :last] += part[:, :last]
            over = lane >= LANES - r
            acc_ref[:, last:] += jnp.where(over, 0.0, part[:, last:])
            before_ref[...] += jnp.where(over, part[:, last:], 0.0)
    total = jnp.zeros((nblk, LANES + steps), jnp.float32)
    for q in range(Q1):
        rows = slice(nblk * q, nblk * (q + 1))
        total = total + shift_left(
            jnp.concatenate([before_ref[rows, :], acc_ref[rows, :]], axis=1), R1 * q
        )
    out_ref[...] = total[:, LANES:]
    if sent_ref is not None:
        sent_ref[...] = total[:, LANES - MARGIN : LANES - MARGIN + steps]


def sender_kernel(spectra_hbm, delay_hbm, out_ref, sent_ref, *scratch):
    @pl.when(lax.axis_index("tm") > 0)
    def _():
        own_sums(spectra_hbm, delay_hbm, out_ref, sent_ref, *scratch)


def first_kernel(spectra_hbm, delay_hbm, sums_ref, out_ref, *scratch):
    del sums_ref

    @pl.when(lax.axis_index("tm") == 0)
    def _():
        own_sums(spectra_hbm, delay_hbm, out_ref, None, *scratch)


def ready_kernel(fine_hbm, widths_hbm, selector_ref, triangle_ref, turn_ref, scale_ref, fine_ref, widths_ref, sems):
    copies = [
        pltpu.make_async_copy(fine_hbm, fine_ref, sems.at[0]),
        pltpu.make_async_copy(widths_hbm, widths_ref, sems.at[1]),
    ]
    for copy in copies:
        copy.start()
    length = triangle_ref.shape[0]
    before = lax.broadcasted_iota(jnp.int32, (length, length), 0)
    after = lax.broadcasted_iota(jnp.int32, (length, length), 1)
    triangle_ref[...] = jnp.where(before < after, 1.0, 0.0).astype(jnp.bfloat16)
    for copy in copies:
        copy.wait()
    fine = from_root(fine_ref[...], 1)
    fine = jnp.concatenate([fine - r for r in range(R2)], axis=1).astype(jnp.bfloat16)
    selector_ref[...] = jnp.concatenate([one_hot(fine, float(R2 * q)) for q in range(Q2)], axis=0)
    lane = lax.broadcasted_iota(jnp.int32, (1, LANES), 1)
    for index in range(turn_ref.shape[0]):
        width = jnp.full((1, LANES), widths_ref[index])
        turn_ref[index : index + 1, :] = (lane + width) & (LANES - 1)
        scale_ref[index : index + 1, :] = 1.0 / jnp.sqrt(width.astype(jnp.float32))


def join_kernel(own_ref, next_ref, ready_ref, out_ref, rows_ref):
    del ready_ref
    nblk, steps = own_ref.shape
    left = steps - MARGIN - LANES
    total = jnp.concatenate(
        [
            jnp.zeros((nblk, left), jnp.float32),
            next_ref[...],
            jnp.zeros((nblk, 3 * LANES - left - steps), jnp.float32),
        ],
        axis=1,
    )
    rows_ref[pl.ds(0, nblk, stride=CHUNKS), :] = own_ref[:, :LANES]
    rows_ref[pl.ds(1, nblk, stride=CHUNKS), :] = own_ref[:, LANES:] + total[:, :LANES]
    rows_ref[pl.ds(2, nblk, stride=CHUNKS), :] = total[:, LANES : 2 * LANES]
    rows_ref[pl.ds(3, nblk, stride=CHUNKS), :] = total[:, 2 * LANES :]
    out_ref[...] = rows_ref[...].astype(jnp.bfloat16)


def trial_kernel(sub_ref, selector_ref, triangle_ref, turn_ref, scale_ref, out_ref, rows_ref):
    trials = out_ref.shape[1]
    nsub = sub_ref.shape[0] // CHUNKS
    rows_ref[...] = sub_ref[...].astype(jnp.float32)
    sub = jnp.concatenate(
        [rows_ref[pl.ds(m, nsub, stride=CHUNKS), :] for m in range(CHUNKS)], axis=1
    ).astype(jnp.bfloat16)
    shifted = jnp.concatenate([shift_left(sub, r) for r in range(R2)], axis=0)
    parts = jnp.dot(selector_ref[...], shifted, preferred_element_type=jnp.float32)
    series = parts[:trials]
    for q in range(1, Q2):
        series = series + shift_left(parts[trials * q : trials * (q + 1)], R2 * q)
    series = series[:, : triangle_ref.shape[0]] * (1.0 / math.sqrt(CHANNELS))
    high = series.astype(jnp.bfloat16)
    rest = series - high.astype(jnp.float32)
    middle = rest.astype(jnp.bfloat16)
    low = (rest - middle.astype(jnp.float32)).astype(jnp.bfloat16)
    sums = jnp.dot(
        jnp.concatenate([high, middle, low], axis=0),
        triangle_ref[...],
        preferred_element_type=jnp.float32,
    )
    prefix = sums[:trials] + (sums[trials : 2 * trials] + sums[2 * trials :])
    columns = [prefix[:, LANES * m : LANES * (m + 1)] for m in range(3)]
    lane = lax.broadcasted_iota(jnp.int32, (trials, LANES), 1)
    for index in range(out_ref.shape[0]):
        turn = jnp.broadcast_to(turn_ref[index : index + 1, :], (trials, LANES))
        scale = jnp.broadcast_to(scale_ref[index : index + 1, :], (trials, LANES))
        turned = [jnp.take_along_axis(column, turn, axis=1) for column in columns]
        inside = turn > lane
        for m in range(2):
            upper = jnp.where(inside, turned[m], turned[m + 1])
            out_ref[index, :, LANES * m : LANES * (m + 1)] = (
                (upper - columns[m]) * scale
            ).astype(jnp.bfloat16)


VMEM = pl.BlockSpec(memory_space=pltpu.VMEM)
HBM = pl.BlockSpec(memory_space=pltpu.HBM)
PARAMS = pltpu.CompilerParams(vmem_limit_bytes=16 * 1024 * 1024)


def per_device(spectra, coarse_delay, fine_delay, widths):
    channels, steps = spectra.shape
    nblk = coarse_delay.shape[1]
    nsub, _, trials = fine_delay.shape
    count = widths.shape[0]
    length = steps + WMAX
    by_block = coarse_delay.T
    fine = fine_delay.reshape(nsub, trials).T
    block = jax.ShapeDtypeStruct((nblk, steps), jnp.float32)
    scratch = [
        pltpu.VMEM(spectra.shape, spectra.dtype),
        pltpu.VMEM(by_block.shape, by_block.dtype),
        pltpu.VMEM((Q1 * nblk, steps), jnp.float32),
        pltpu.VMEM((Q1 * nblk, LANES), jnp.float32),
        pltpu.SemaphoreType.DMA((2,)),
    ]
    sources = [pltpu.with_memory_space_constraint(x, pltpu.HBM) for x in (spectra, by_block)]
    own, sent = pl.pallas_call(
        sender_kernel,
        out_shape=[block] * 2,
        in_specs=[HBM] * 2,
        out_specs=[VMEM] * 2,
        scratch_shapes=scratch,
        compiler_params=PARAMS,
        name="sender_sums",
    )(*sources)
    blocks = lax.axis_size("tm")
    following = lax.ppermute(sent, "tm", [(z + 1, z) for z in range(blocks - 1)])
    own = pl.pallas_call(
        first_kernel,
        out_shape=block,
        in_specs=[HBM] * 2 + [VMEM],
        out_specs=VMEM,
        scratch_shapes=scratch,
        input_output_aliases={2: 0},
        compiler_params=PARAMS,
        cost_estimate=pl.CostEstimate(flops=1 << 30, bytes_accessed=1 << 20, transcendentals=0),
        name="first_sums",
    )(*sources, own)
    selector, triangle, turn, scale = pl.pallas_call(
        ready_kernel,
        out_shape=[
            jax.ShapeDtypeStruct((Q2 * trials, R2 * nsub), jnp.bfloat16),
            jax.ShapeDtypeStruct((length, length), jnp.bfloat16),
            jax.ShapeDtypeStruct((count, LANES), jnp.int32),
            jax.ShapeDtypeStruct((count, LANES), jnp.float32),
        ],
        in_specs=[HBM] * 2,
        out_specs=[VMEM] * 4,
        scratch_shapes=[
            pltpu.VMEM(fine.shape, fine.dtype),
            pltpu.SMEM(widths.shape, widths.dtype),
            pltpu.SemaphoreType.DMA((2,)),
        ],
        compiler_params=PARAMS,
        cost_estimate=pl.CostEstimate(flops=1 << 30, bytes_accessed=1 << 20, transcendentals=0),
        name="ready",
    )(*(pltpu.with_memory_space_constraint(x, pltpu.HBM) for x in (fine, widths)))
    subbands = pl.pallas_call(
        join_kernel,
        out_shape=jax.ShapeDtypeStruct((nblk * CHUNKS, LANES), jnp.bfloat16),
        in_specs=[VMEM] * 3,
        out_specs=VMEM,
        scratch_shapes=[pltpu.VMEM((nblk * CHUNKS, LANES), jnp.float32)],
        compiler_params=PARAMS,
        name="join",
    )(own, following, turn)
    groups = lax.axis_size("chan")
    received = lax.all_to_all(
        subbands,
        "chan",
        split_axis=0,
        concat_axis=0,
        tiled=True,
        axis_index_groups=[[(i + ROOT) % groups for i in range(groups)]],
    )
    return pl.pallas_call(
        trial_kernel,
        out_shape=jax.ShapeDtypeStruct((count, trials, steps), jnp.bfloat16),
        in_specs=[VMEM] * 5,
        out_specs=VMEM,
        scratch_shapes=[pltpu.VMEM((nsub * CHUNKS, LANES), jnp.float32)],
        compiler_params=PARAMS,
        name="trials",
    )(received, selector, triangle, turn, scale)


def solution(mesh):
    return jax.shard_map(
        per_device,
        mesh=mesh,
        in_specs=(P("chan", "tm"), P("chan", None), P(None, "chan", None), P()),
        out_specs=P(None, "chan", "tm"),
        check_vma=False,
    )
```

```python
import functools
import math

import jax
import jax.numpy as jnp
from jax import lax
from jax.experimental import pallas as pl
from jax.experimental.pallas import tpu as pltpu
from jax.sharding import PartitionSpec as P

CHANNELS = 16384
D1MAX = 95
D2MAX = 31
WMAX = 128
LANES = 128
MARGIN = D1MAX + 1
R1 = 16
Q1 = (D1MAX + 1) // R1
R2 = 4
Q2 = (D2MAX + 1) // R2
ROOT = 41
CHUNKS = 4


def shift_left(x, by):
    if by == 0:
        return x
    return jnp.concatenate([x[:, by:], jnp.zeros((x.shape[0], by), x.dtype)], axis=1)


def turn_left(x, by):
    if by == 0:
        return x
    return jnp.concatenate([x[:, by:], x[:, :by]], axis=1)


def from_root(x, axis):
    first, second = jnp.split(x, [ROOT], axis=axis)
    return jnp.concatenate([second, first], axis=axis)


def one_hot(delay, level):
    return jnp.where(delay == level, jnp.ones((), jnp.bfloat16), jnp.zeros((), jnp.bfloat16))


def own_sums(
    spectra_hbm, delay_hbm, out_ref, sent_ref,
    spectra_ref, delay_ref, acc_ref, before_ref, sems,
):
    copies = [
        pltpu.make_async_copy(spectra_hbm, spectra_ref, sems.at[0]),
        pltpu.make_async_copy(delay_hbm, delay_ref, sems.at[1]),
    ]
    for copy in copies:
        copy.start()
    for copy in copies:
        copy.wait()
    nblk, steps = out_ref.shape
    last = steps - LANES
    spectra = spectra_ref[...]
    delay = from_root(delay_ref[...], 0).astype(jnp.bfloat16)
    lane = lax.broadcasted_iota(jnp.int32, (1, LANES), 1)
    for r in range(R1):
        selector = jnp.concatenate([one_hot(delay, float(R1 * q + r)) for q in range(Q1)], axis=0)
        part = jnp.dot(selector, turn_left(spectra, r), preferred_element_type=jnp.float32)
        if r == 0:
            acc_ref[...] = part
            continue
        acc_ref[...] += part
        over = jnp.where(lane >= LANES - r, part[:, last:], 0.0)
        if r == 1:
            before_ref[...] = over
        else:
            before_ref[...] += over
    total = jnp.zeros((nblk, LANES + steps), jnp.float32)
    for q in range(Q1):
        rows = slice(nblk * q, nblk * (q + 1))
        over = before_ref[rows, :]
        total = total + shift_left(
            jnp.concatenate([over, acc_ref[rows, :last], acc_ref[rows, last:] - over], axis=1),
            R1 * q,
        )
    out_ref[...] = total[:, LANES:]
    if sent_ref is not None:
        sent_ref[...] = total[:, LANES - MARGIN : LANES - MARGIN + steps].astype(jnp.bfloat16)


def sender_kernel(spectra_hbm, delay_hbm, out_ref, sent_ref, *scratch):
    @pl.when(lax.axis_index("tm") > 0)
    def _():
        own_sums(spectra_hbm, delay_hbm, out_ref, sent_ref, *scratch)


def first_kernel(spectra_hbm, delay_hbm, sums_ref, out_ref, *scratch):
    del sums_ref

    @pl.when(lax.axis_index("tm") == 0)
    def _():
        own_sums(spectra_hbm, delay_hbm, out_ref, None, *scratch)


def ready_kernel(fine_hbm, widths_hbm, selector_ref, band_ref, scale_ref, fine_ref, widths_ref, sems):
    copies = [
        pltpu.make_async_copy(fine_hbm, fine_ref, sems.at[0]),
        pltpu.make_async_copy(widths_hbm, widths_ref, sems.at[1]),
    ]
    for copy in copies:
        copy.start()
    for copy in copies:
        copy.wait()
    fine = from_root(fine_ref[...], 1)
    fine = jnp.concatenate([fine - r for r in range(R2)], axis=1).astype(jnp.bfloat16)
    selector_ref[...] = jnp.concatenate([one_hot(fine, float(R2 * q)) for q in range(Q2)], axis=0)
    shape = (band_ref.shape[0], LANES)
    ahead = lax.broadcasted_iota(jnp.int32, shape, 0) - lax.broadcasted_iota(jnp.int32, shape, 1)
    for index in range(scale_ref.shape[0]):
        width = widths_ref[index]
        counts = jnp.logical_and(ahead >= 0, ahead < width)
        band_ref[:, LANES * index : LANES * (index + 1)] = jnp.where(counts, 1.0, 0.0).astype(jnp.bfloat16)
        scale_ref[index : index + 1, :] = 1.0 / jnp.sqrt(
            jnp.full((1, LANES), width).astype(jnp.float32)
        )


def join_kernel(own_ref, next_ref, ready_ref, out_ref, rows_ref):
    del ready_ref
    nblk, steps = own_ref.shape
    left = steps - MARGIN - LANES
    total = jnp.concatenate(
        [
            jnp.zeros((nblk, left), jnp.float32),
            next_ref[...].astype(jnp.float32),
            jnp.zeros((nblk, 3 * LANES - left - steps), jnp.float32),
        ],
        axis=1,
    )
    rows_ref[pl.ds(0, nblk, stride=CHUNKS), :] = own_ref[:, :LANES]
    rows_ref[pl.ds(1, nblk, stride=CHUNKS), :] = own_ref[:, LANES:] + total[:, :LANES]
    rows_ref[pl.ds(2, nblk, stride=CHUNKS), :] = total[:, LANES : 2 * LANES]
    rows_ref[pl.ds(3, nblk, stride=CHUNKS), :] = total[:, 2 * LANES :]
    out_ref[...] = rows_ref[...].astype(jnp.bfloat16)


def trial_kernel(sub_ref, selector_ref, band_ref, scale_ref, out_ref, rows_ref):
    count, trials, steps = out_ref.shape
    nsub = sub_ref.shape[0] // CHUNKS
    rows_ref[...] = sub_ref[...].astype(jnp.float32)
    sub = jnp.concatenate(
        [rows_ref[pl.ds(m, nsub, stride=CHUNKS), :] for m in range(CHUNKS)], axis=1
    ).astype(jnp.bfloat16)
    shifted = jnp.concatenate([shift_left(sub, r) for r in range(R2)], axis=0)
    parts = jnp.dot(selector_ref[...], shifted, preferred_element_type=jnp.float32)
    series = parts[:trials]
    for q in range(1, Q2):
        series = series + shift_left(parts[trials * q : trials * (q + 1)], R2 * q)
    series = series[:, : steps + WMAX] * (1.0 / math.sqrt(CHANNELS))
    high = series.astype(jnp.bfloat16)
    rest = series - high.astype(jnp.float32)
    middle = rest.astype(jnp.bfloat16)
    low = (rest - middle.astype(jnp.float32)).astype(jnp.bfloat16)
    terms = (high, middle, low)
    reach = band_ref.shape[0]
    halves = range(0, steps, LANES)
    windows = jnp.concatenate([term[:, t : t + reach] for t in halves for term in terms], axis=0)
    sums = jnp.dot(windows, band_ref[...], preferred_element_type=jnp.float32)
    sums = sums.reshape(len(halves), len(terms), trials, count * LANES)
    for index in range(count):
        columns = slice(LANES * index, LANES * (index + 1))
        scale = scale_ref[index : index + 1, :]
        for half, t in enumerate(halves):
            first, second, third = (sums[half, term, :, columns] for term in range(len(terms)))
            out_ref[index, :, t : t + LANES] = ((first + (second + third)) * scale).astype(jnp.bfloat16)


VMEM = pl.BlockSpec(memory_space=pltpu.VMEM)
HBM = pl.BlockSpec(memory_space=pltpu.HBM)
PARAMS = pltpu.CompilerParams(vmem_limit_bytes=16 * 1024 * 1024)


def per_device(spectra, coarse_delay, fine_delay, widths):
    channels, steps = spectra.shape
    nblk = coarse_delay.shape[1]
    nsub, _, trials = fine_delay.shape
    count = widths.shape[0]
    by_block = coarse_delay.T
    fine = fine_delay.reshape(nsub, trials).T
    block = jax.ShapeDtypeStruct((nblk, steps), jnp.float32)
    scratch = [
        pltpu.VMEM(spectra.shape, spectra.dtype),
        pltpu.VMEM(by_block.shape, by_block.dtype),
        pltpu.VMEM((Q1 * nblk, steps), jnp.float32),
        pltpu.VMEM((Q1 * nblk, LANES), jnp.float32),
        pltpu.SemaphoreType.DMA((2,)),
    ]
    sources = [pltpu.with_memory_space_constraint(x, pltpu.HBM) for x in (spectra, by_block)]
    own, sent = pl.pallas_call(
        sender_kernel,
        out_shape=[block, jax.ShapeDtypeStruct((nblk, steps), jnp.bfloat16)],
        in_specs=[HBM] * 2,
        out_specs=[VMEM] * 2,
        scratch_shapes=scratch,
        compiler_params=PARAMS,
        name="sender_sums",
    )(*sources)
    blocks = lax.axis_size("tm")
    following = lax.ppermute(sent, "tm", [(z + 1, z) for z in range(blocks - 1)])
    own = pl.pallas_call(
        first_kernel,
        out_shape=block,
        in_specs=[HBM] * 2 + [VMEM],
        out_specs=VMEM,
        scratch_shapes=scratch,
        input_output_aliases={2: 0},
        compiler_params=PARAMS,
        cost_estimate=pl.CostEstimate(flops=1 << 30, bytes_accessed=1 << 20, transcendentals=0),
        name="first_sums",
    )(*sources, own)
    selector, band, scale = pl.pallas_call(
        ready_kernel,
        out_shape=[
            jax.ShapeDtypeStruct((Q2 * trials, R2 * nsub), jnp.bfloat16),
            jax.ShapeDtypeStruct((LANES + WMAX, count * LANES), jnp.bfloat16),
            jax.ShapeDtypeStruct((count, LANES), jnp.float32),
        ],
        in_specs=[HBM] * 2,
        out_specs=[VMEM] * 3,
        scratch_shapes=[
            pltpu.VMEM(fine.shape, fine.dtype),
            pltpu.SMEM(widths.shape, widths.dtype),
            pltpu.SemaphoreType.DMA((2,)),
        ],
        compiler_params=PARAMS,
        cost_estimate=pl.CostEstimate(flops=1 << 30, bytes_accessed=1 << 20, transcendentals=0),
        name="ready",
    )(*(pltpu.with_memory_space_constraint(x, pltpu.HBM) for x in (fine, widths)))
    subbands = pl.pallas_call(
        join_kernel,
        out_shape=jax.ShapeDtypeStruct((nblk * CHUNKS, LANES), jnp.bfloat16),
        in_specs=[VMEM] * 3,
        out_specs=VMEM,
        scratch_shapes=[pltpu.VMEM((nblk * CHUNKS, LANES), jnp.float32)],
        compiler_params=PARAMS,
        name="join",
    )(own, following, scale)
    groups = lax.axis_size("chan")
    received = lax.all_to_all(
        subbands,
        "chan",
        split_axis=0,
        concat_axis=0,
        tiled=True,
        axis_index_groups=[[(i + ROOT) % groups for i in range(groups)]],
    )
    return pl.pallas_call(
        trial_kernel,
        out_shape=jax.ShapeDtypeStruct((count, trials, steps), jnp.bfloat16),
        in_specs=[VMEM] * 4,
        out_specs=VMEM,
        scratch_shapes=[pltpu.VMEM((nsub * CHUNKS, LANES), jnp.float32)],
        compiler_params=PARAMS,
        name="trials",
    )(received, selector, band, scale)


def solution(mesh):
    return jax.shard_map(
        per_device,
        mesh=mesh,
        in_specs=(P("chan", "tm"), P("chan", None), P(None, "chan", None), P()),
        out_specs=P(None, "chan", "tm"),
        check_vma=False,
    )
```

```python
import functools
import math

import jax
import jax.numpy as jnp
from jax import lax
from jax.experimental import pallas as pl
from jax.experimental.pallas import tpu as pltpu
from jax.sharding import PartitionSpec as P

CHANNELS = 16384
D1MAX = 95
D2MAX = 31
WMAX = 128
LANES = 128
MARGIN = D1MAX + 1
R1 = 16
Q1 = (D1MAX + 1) // R1
R2 = 4
Q2 = (D2MAX + 1) // R2
BASE = 42
CHUNKS = 4


def shift_left(x, by):
    if by == 0:
        return x
    return jnp.concatenate([x[:, by:], jnp.zeros((x.shape[0], by), x.dtype)], axis=1)


def turn_left(x, by):
    if by == 0:
        return x
    return jnp.concatenate([x[:, by:], x[:, :by]], axis=1)


def listed(i, count):
    return (i + BASE) % count ^ 1


def in_listed_order(x):
    count = x.shape[0]
    x = jnp.concatenate([x[BASE:], x[:BASE]], axis=0)
    even = lax.broadcasted_iota(jnp.int32, x.shape, 0) % 2 == 0
    return jnp.where(even, pltpu.roll(x, count - 1, 0), pltpu.roll(x, 1, 0))


def one_hot(delay, level):
    return jnp.where(delay == level, jnp.ones((), jnp.bfloat16), jnp.zeros((), jnp.bfloat16))


def own_sums(
    spectra_hbm, delay_hbm, out_ref, sent_ref,
    spectra_ref, delay_ref, acc_ref, before_ref, sems,
):
    copies = [
        pltpu.make_async_copy(spectra_hbm, spectra_ref, sems.at[0]),
        pltpu.make_async_copy(delay_hbm, delay_ref, sems.at[1]),
    ]
    for copy in copies:
        copy.start()
    for copy in copies:
        copy.wait()
    nblk, steps = out_ref.shape
    last = steps - LANES
    spectra = spectra_ref[...]
    delay = in_listed_order(delay_ref[...]).astype(jnp.bfloat16)
    lane = lax.broadcasted_iota(jnp.int32, (1, LANES), 1)
    for r in range(R1):
        selector = jnp.concatenate([one_hot(delay, float(R1 * q + r)) for q in range(Q1)], axis=0)
        part = jnp.dot(selector, turn_left(spectra, r), preferred_element_type=jnp.float32)
        if r == 0:
            acc_ref[...] = part
            continue
        acc_ref[...] += part
        over = jnp.where(lane >= LANES - r, part[:, last:], 0.0)
        if r == 1:
            before_ref[...] = over
        else:
            before_ref[...] += over
    total = jnp.zeros((nblk, LANES + steps), jnp.float32)
    for q in range(Q1):
        rows = slice(nblk * q, nblk * (q + 1))
        over = before_ref[rows, :]
        total = total + shift_left(
            jnp.concatenate([over, acc_ref[rows, :last], acc_ref[rows, last:] - over], axis=1),
            R1 * q,
        )
    out_ref[...] = total[:, LANES:]
    if sent_ref is not None:
        around = jnp.where(lane < LANES - MARGIN, total[:, 2 * LANES :], total[:, :LANES])
        sent_ref[...] = jnp.concatenate([total[:, LANES : 2 * LANES], around], axis=1).astype(
            jnp.bfloat16
        )


def sender_kernel(spectra_hbm, delay_hbm, out_ref, sent_ref, *scratch):
    @pl.when(lax.axis_index("tm") > 0)
    def _():
        own_sums(spectra_hbm, delay_hbm, out_ref, sent_ref, *scratch)


def first_kernel(spectra_hbm, delay_hbm, sums_ref, out_ref, *scratch):
    del sums_ref

    @pl.when(lax.axis_index("tm") == 0)
    def _():
        own_sums(spectra_hbm, delay_hbm, out_ref, None, *scratch)


def ready_kernel(fine_hbm, widths_hbm, selector_ref, band_ref, scale_ref, fine_ref, widths_ref, sems):
    copies = [
        pltpu.make_async_copy(fine_hbm, fine_ref, sems.at[0]),
        pltpu.make_async_copy(widths_hbm, widths_ref, sems.at[1]),
    ]
    for copy in copies:
        copy.start()
    for copy in copies:
        copy.wait()
    nsub = fine_ref.shape[1]
    subband = lax.broadcasted_iota(jnp.int32, (nsub, nsub), 0)
    place = lax.broadcasted_iota(jnp.int32, (nsub, nsub), 1)
    place = 2 * (place % (nsub // 2)) + place // (nsub // 2)
    order = jnp.where(subband == listed(place, nsub), 1.0, 0.0).astype(jnp.bfloat16)
    fine = jnp.dot(fine_ref[...].astype(jnp.bfloat16), order, preferred_element_type=jnp.float32)
    fine = jnp.concatenate([fine - r for r in range(R2)], axis=1).astype(jnp.bfloat16)
    selector_ref[...] = jnp.concatenate([one_hot(fine, float(R2 * q)) for q in range(Q2)], axis=0)
    shape = (band_ref.shape[0], LANES)
    ahead = lax.broadcasted_iota(jnp.int32, shape, 0) - lax.broadcasted_iota(jnp.int32, shape, 1)
    for index in range(scale_ref.shape[0]):
        width = widths_ref[index]
        counts = jnp.logical_and(ahead >= 0, ahead < width)
        band_ref[:, LANES * index : LANES * (index + 1)] = jnp.where(counts, 1.0, 0.0).astype(jnp.bfloat16)
        scale_ref[index : index + 1, :] = 1.0 / jnp.sqrt(
            jnp.full((1, LANES), width).astype(jnp.float32)
        )


def join_kernel(own_ref, next_ref, ready_ref, out_ref, rows_ref):
    del ready_ref
    nblk = own_ref.shape[0]
    following = next_ref[...].astype(jnp.float32)
    chunks = [own_ref[:, :LANES], own_ref[:, LANES:], following[:, :LANES], following[:, LANES:]]
    for m, chunk in enumerate(chunks):
        rows_ref[pl.ds(m, nblk, stride=CHUNKS), :] = chunk
    out_ref[...] = rows_ref[...].astype(jnp.bfloat16)


def trial_kernel(sub_ref, selector_ref, band_ref, scale_ref, out_ref, rows_ref):
    count, trials, steps = out_ref.shape
    nsub = sub_ref.shape[0] // CHUNKS
    rows_ref[...] = sub_ref[...].astype(jnp.float32)

    def chunk(m, first, second):
        return jnp.concatenate(
            [rows_ref[pl.ds(CHUNKS * odd + m, nsub // 2, stride=2 * CHUNKS), :] for odd in (first, second)],
            axis=0,
        )

    around = chunk(3, 1, 0)
    lane = lax.broadcasted_iota(jnp.int32, around.shape, 1)
    sub = jnp.concatenate(
        [
            chunk(0, 0, 1),
            chunk(1, 0, 1) + jnp.where(lane < LANES - MARGIN, 0.0, around),
            chunk(2, 1, 0),
            around,
        ],
        axis=1,
    ).astype(jnp.bfloat16)
    shifted = jnp.concatenate([shift_left(sub, r) for r in range(R2)], axis=0)
    parts = jnp.dot(selector_ref[...], shifted, preferred_element_type=jnp.float32)
    series = parts[:trials]
    for q in range(1, Q2):
        series = series + shift_left(parts[trials * q : trials * (q + 1)], R2 * q)
    series = series[:, : steps + WMAX] * (1.0 / math.sqrt(CHANNELS))
    high = series.astype(jnp.bfloat16)
    rest = series - high.astype(jnp.float32)
    middle = rest.astype(jnp.bfloat16)
    low = (rest - middle.astype(jnp.float32)).astype(jnp.bfloat16)
    terms = (high, middle, low)
    reach = band_ref.shape[0]
    halves = range(0, steps, LANES)
    windows = jnp.concatenate([term[:, t : t + reach] for t in halves for term in terms], axis=0)
    sums = jnp.dot(windows, band_ref[...], preferred_element_type=jnp.float32)
    sums = sums.reshape(len(halves), len(terms), trials, count * LANES)
    for index in range(count):
        columns = slice(LANES * index, LANES * (index + 1))
        scale = scale_ref[index : index + 1, :]
        for half, t in enumerate(halves):
            first, second, third = (sums[half, term, :, columns] for term in range(len(terms)))
            out_ref[index, :, t : t + LANES] = ((first + (second + third)) * scale).astype(jnp.bfloat16)


VMEM = pl.BlockSpec(memory_space=pltpu.VMEM)
HBM = pl.BlockSpec(memory_space=pltpu.HBM)
PARAMS = pltpu.CompilerParams(vmem_limit_bytes=16 * 1024 * 1024)


def per_device(spectra, coarse_delay, fine_delay, widths):
    channels, steps = spectra.shape
    nblk = coarse_delay.shape[1]
    nsub, _, trials = fine_delay.shape
    count = widths.shape[0]
    by_block = coarse_delay.T
    fine = fine_delay.reshape(nsub, trials).T
    block = jax.ShapeDtypeStruct((nblk, steps), jnp.float32)
    scratch = [
        pltpu.VMEM(spectra.shape, spectra.dtype),
        pltpu.VMEM(by_block.shape, by_block.dtype),
        pltpu.VMEM((Q1 * nblk, steps), jnp.float32),
        pltpu.VMEM((Q1 * nblk, LANES), jnp.float32),
        pltpu.SemaphoreType.DMA((2,)),
    ]
    sources = [pltpu.with_memory_space_constraint(x, pltpu.HBM) for x in (spectra, by_block)]
    own, sent = pl.pallas_call(
        sender_kernel,
        out_shape=[block, jax.ShapeDtypeStruct((nblk, steps), jnp.bfloat16)],
        in_specs=[HBM] * 2,
        out_specs=[VMEM] * 2,
        scratch_shapes=scratch,
        compiler_params=PARAMS,
        name="sender_sums",
    )(*sources)
    blocks = lax.axis_size("tm")
    groups = lax.axis_size("chan")
    following = lax.ppermute(
        sent,
        ("chan", "tm"),
        [
            (c * blocks + z + 1, (c ^ 1) * blocks + z)
            for c in range(groups)
            for z in range(blocks - 1)
        ],
    )
    own = pl.pallas_call(
        first_kernel,
        out_shape=block,
        in_specs=[HBM] * 2 + [VMEM],
        out_specs=VMEM,
        scratch_shapes=scratch,
        input_output_aliases={2: 0},
        compiler_params=PARAMS,
        cost_estimate=pl.CostEstimate(flops=1 << 30, bytes_accessed=1 << 20, transcendentals=0),
        name="first_sums",
    )(*sources, own)
    selector, band, scale = pl.pallas_call(
        ready_kernel,
        out_shape=[
            jax.ShapeDtypeStruct((Q2 * trials, R2 * nsub), jnp.bfloat16),
            jax.ShapeDtypeStruct((LANES + WMAX, count * LANES), jnp.bfloat16),
            jax.ShapeDtypeStruct((count, LANES), jnp.float32),
        ],
        in_specs=[HBM] * 2,
        out_specs=[VMEM] * 3,
        scratch_shapes=[
            pltpu.VMEM(fine.shape, fine.dtype),
            pltpu.SMEM(widths.shape, widths.dtype),
            pltpu.SemaphoreType.DMA((2,)),
        ],
        compiler_params=PARAMS,
        cost_estimate=pl.CostEstimate(flops=1 << 30, bytes_accessed=1 << 20, transcendentals=0),
        name="ready",
    )(*(pltpu.with_memory_space_constraint(x, pltpu.HBM) for x in (fine, widths)))
    subbands = pl.pallas_call(
        join_kernel,
        out_shape=jax.ShapeDtypeStruct((nblk * CHUNKS, LANES), jnp.bfloat16),
        in_specs=[VMEM] * 3,
        out_specs=VMEM,
        scratch_shapes=[pltpu.VMEM((nblk * CHUNKS, LANES), jnp.float32)],
        compiler_params=PARAMS,
        name="join",
    )(own, following, scale)
    received = lax.all_to_all(
        subbands,
        "chan",
        split_axis=0,
        concat_axis=0,
        tiled=True,
        axis_index_groups=[[listed(i, groups) for i in range(groups)]],
    )
    return pl.pallas_call(
        trial_kernel,
        out_shape=jax.ShapeDtypeStruct((count, trials, steps), jnp.bfloat16),
        in_specs=[VMEM] * 4,
        out_specs=VMEM,
        scratch_shapes=[pltpu.VMEM((nsub * CHUNKS, LANES), jnp.float32)],
        compiler_params=PARAMS,
        name="trials",
    )(received, selector, band, scale)


def solution(mesh):
    return jax.shard_map(
        per_device,
        mesh=mesh,
        in_specs=(P("chan", "tm"), P("chan", None), P(None, "chan", None), P()),
        out_specs=P(None, "chan", "tm"),
        check_vma=False,
    )
```

```python
import functools
import math

import jax
import jax.numpy as jnp
from jax import lax
from jax.experimental import pallas as pl
from jax.experimental.pallas import tpu as pltpu
from jax.sharding import PartitionSpec as P

CHANNELS = 16384
D1MAX = 95
D2MAX = 31
WMAX = 128
LANES = 128
MARGIN = D1MAX + 1
R1 = 16
Q1 = (D1MAX + 1) // R1
R2 = 4
Q2 = (D2MAX + 1) // R2
BASE = 42
CHUNKS = 4


def shift_left(x, by):
    if by == 0:
        return x
    return jnp.concatenate([x[:, by:], jnp.zeros((x.shape[0], by), x.dtype)], axis=1)


def turn_left(x, by):
    if by == 0:
        return x
    return jnp.concatenate([x[:, by:], x[:, :by]], axis=1)


def listed(i, count):
    return (i + BASE) % count ^ 1


def in_listed_order(x):
    count = x.shape[0]
    x = jnp.concatenate([x[BASE:], x[:BASE]], axis=0)
    even = lax.broadcasted_iota(jnp.int32, x.shape, 0) % 2 == 0
    return jnp.where(even, pltpu.roll(x, count - 1, 0), pltpu.roll(x, 1, 0))


def one_hot(delay, level):
    return jnp.where(delay == level, jnp.ones((), jnp.bfloat16), jnp.zeros((), jnp.bfloat16))


def own_sums(
    spectra_hbm, delay_hbm, out_ref, sent_ref,
    spectra_ref, delay_ref, acc_ref, before_ref, sems,
):
    copies = []
    for source, target, cuts in ((delay_hbm, delay_ref, 2), (spectra_hbm, spectra_ref, 4)):
        rows = source.shape[0] // cuts
        for cut in range(cuts):
            part = pl.ds(rows * cut, rows)
            copies.append(
                pltpu.make_async_copy(source.at[part], target.at[part], sems.at[len(copies)])
            )
    for copy in copies:
        copy.start()
    for copy in copies:
        copy.wait()
    nblk, steps = out_ref.shape
    last = steps - LANES
    spectra = spectra_ref[...]
    delay = in_listed_order(delay_ref[...]).astype(jnp.bfloat16)
    lane = lax.broadcasted_iota(jnp.int32, (1, LANES), 1)
    for r in range(R1):
        selector = jnp.concatenate([one_hot(delay, float(R1 * q + r)) for q in range(Q1)], axis=0)
        part = jnp.dot(selector, turn_left(spectra, r), preferred_element_type=jnp.float32)
        if r == 0:
            acc_ref[...] = part
            continue
        acc_ref[...] += part
        over = jnp.where(lane >= LANES - r, part[:, last:], 0.0)
        if r == 1:
            before_ref[...] = over
        else:
            before_ref[...] += over
    total = jnp.zeros((nblk, LANES + steps), jnp.float32)
    for q in range(Q1):
        rows = slice(nblk * q, nblk * (q + 1))
        over = before_ref[rows, :]
        total = total + shift_left(
            jnp.concatenate([over, acc_ref[rows, :last], acc_ref[rows, last:] - over], axis=1),
            R1 * q,
        )
    out_ref[...] = total[:, LANES:]
    if sent_ref is not None:
        around = jnp.where(lane < LANES - MARGIN, total[:, 2 * LANES :], total[:, :LANES])
        sent_ref[...] = jnp.concatenate([total[:, LANES : 2 * LANES], around], axis=1).astype(
            jnp.bfloat16
        )


def sender_kernel(spectra_hbm, delay_hbm, out_ref, sent_ref, *scratch):
    @pl.when(lax.axis_index("tm") > 0)
    def _():
        own_sums(spectra_hbm, delay_hbm, out_ref, sent_ref, *scratch)


def first_kernel(spectra_hbm, delay_hbm, sums_ref, out_ref, *scratch):
    del sums_ref

    @pl.when(lax.axis_index("tm") == 0)
    def _():
        own_sums(spectra_hbm, delay_hbm, out_ref, None, *scratch)


def ready_kernel(fine_hbm, widths_hbm, selector_ref, band_ref, scale_ref, fine_ref, widths_ref, sems):
    copies = [
        pltpu.make_async_copy(fine_hbm, fine_ref, sems.at[0]),
        pltpu.make_async_copy(widths_hbm, widths_ref, sems.at[1]),
    ]
    for copy in copies:
        copy.start()
    for copy in copies:
        copy.wait()
    nsub = fine_ref.shape[1]
    subband = lax.broadcasted_iota(jnp.int32, (nsub, nsub), 0)
    place = lax.broadcasted_iota(jnp.int32, (nsub, nsub), 1)
    place = 2 * (place % (nsub // 2)) + place // (nsub // 2)
    order = jnp.where(subband == listed(place, nsub), 1.0, 0.0).astype(jnp.bfloat16)
    fine = jnp.dot(fine_ref[...].astype(jnp.bfloat16), order, preferred_element_type=jnp.float32)
    fine = jnp.concatenate([fine - r for r in range(R2)], axis=1).astype(jnp.bfloat16)
    selector_ref[...] = jnp.concatenate([one_hot(fine, float(R2 * q)) for q in range(Q2)], axis=0)
    shape = (band_ref.shape[0], LANES)
    ahead = lax.broadcasted_iota(jnp.int32, shape, 0) - lax.broadcasted_iota(jnp.int32, shape, 1)
    for index in range(scale_ref.shape[0]):
        width = widths_ref[index]
        counts = jnp.logical_and(ahead >= 0, ahead < width)
        band_ref[:, LANES * index : LANES * (index + 1)] = jnp.where(counts, 1.0, 0.0).astype(jnp.bfloat16)
        scale_ref[index : index + 1, :] = (1.0 / math.sqrt(CHANNELS)) / jnp.sqrt(
            jnp.full((1, LANES), width).astype(jnp.float32)
        )


def join_kernel(own_ref, next_ref, ready_ref, out_ref, rows_ref):
    del ready_ref
    nblk = own_ref.shape[0]
    following = next_ref[...].astype(jnp.float32)
    chunks = [own_ref[:, :LANES], own_ref[:, LANES:], following[:, :LANES], following[:, LANES:]]
    for m, chunk in enumerate(chunks):
        rows_ref[pl.ds(m, nblk, stride=CHUNKS), :] = chunk
    out_ref[...] = rows_ref[...].astype(jnp.bfloat16)


def trial_kernel(sub_ref, selector_ref, band_ref, scale_ref, out_ref, rows_ref):
    count, trials, steps = out_ref.shape
    nsub = sub_ref.shape[0] // CHUNKS
    rows_ref[...] = sub_ref[...].astype(jnp.float32)

    def chunk(m, first, second):
        return jnp.concatenate(
            [rows_ref[pl.ds(CHUNKS * odd + m, nsub // 2, stride=2 * CHUNKS), :] for odd in (first, second)],
            axis=0,
        )

    around = chunk(3, 1, 0)
    lane = lax.broadcasted_iota(jnp.int32, around.shape, 1)
    sub = jnp.concatenate(
        [
            chunk(0, 0, 1),
            chunk(1, 0, 1) + jnp.where(lane < LANES - MARGIN, 0.0, around),
            chunk(2, 1, 0),
            around,
        ],
        axis=1,
    )
    shifted = jnp.concatenate(
        [turn_left(sub, r).astype(jnp.bfloat16) for r in range(R2)], axis=0
    )
    parts = jnp.dot(selector_ref[...], shifted, preferred_element_type=jnp.float32)
    series = parts[:trials]
    for q in range(1, Q2):
        series = series + shift_left(parts[trials * q : trials * (q + 1)], R2 * q)
    series = series[:, : steps + WMAX]
    high = series.astype(jnp.bfloat16)
    rest = series - high.astype(jnp.float32)
    middle = rest.astype(jnp.bfloat16)
    low = (rest - middle.astype(jnp.float32)).astype(jnp.bfloat16)
    terms = (high, middle, low)
    reach = band_ref.shape[0]
    halves = range(0, steps, LANES)
    windows = jnp.concatenate([term[:, t : t + reach] for t in halves for term in terms], axis=0)
    sums = jnp.dot(windows, band_ref[...], preferred_element_type=jnp.float32)
    sums = sums.reshape(len(halves), len(terms), trials, count * LANES)
    for index in range(count):
        columns = slice(LANES * index, LANES * (index + 1))
        scale = scale_ref[index : index + 1, :]
        for half, t in enumerate(halves):
            first, second, third = (sums[half, term, :, columns] for term in range(len(terms)))
            out_ref[index, :, t : t + LANES] = ((first + (second + third)) * scale).astype(jnp.bfloat16)


VMEM = pl.BlockSpec(memory_space=pltpu.VMEM)
HBM = pl.BlockSpec(memory_space=pltpu.HBM)
PARAMS = pltpu.CompilerParams(vmem_limit_bytes=16 * 1024 * 1024)


def per_device(spectra, coarse_delay, fine_delay, widths):
    channels, steps = spectra.shape
    nblk = coarse_delay.shape[1]
    nsub, _, trials = fine_delay.shape
    count = widths.shape[0]
    by_block = coarse_delay.T
    fine = fine_delay.reshape(nsub, trials).T
    block = jax.ShapeDtypeStruct((nblk, steps), jnp.float32)
    scratch = [
        pltpu.VMEM(spectra.shape, spectra.dtype),
        pltpu.VMEM(by_block.shape, by_block.dtype),
        pltpu.VMEM((Q1 * nblk, steps), jnp.float32),
        pltpu.VMEM((Q1 * nblk, LANES), jnp.float32),
        pltpu.SemaphoreType.DMA((6,)),
    ]
    sources = [pltpu.with_memory_space_constraint(x, pltpu.HBM) for x in (spectra, by_block)]
    own, sent = pl.pallas_call(
        sender_kernel,
        out_shape=[block, jax.ShapeDtypeStruct((nblk, steps), jnp.bfloat16)],
        in_specs=[HBM] * 2,
        out_specs=[VMEM] * 2,
        scratch_shapes=scratch,
        compiler_params=PARAMS,
        name="sender_sums",
    )(*sources)
    blocks = lax.axis_size("tm")
    groups = lax.axis_size("chan")
    following = lax.ppermute(
        sent,
        ("chan", "tm"),
        [
            (c * blocks + z + 1, (c ^ 1) * blocks + z)
            for c in range(groups)
            for z in range(blocks - 1)
        ],
    )
    own = pl.pallas_call(
        first_kernel,
        out_shape=block,
        in_specs=[HBM] * 2 + [VMEM],
        out_specs=VMEM,
        scratch_shapes=scratch,
        input_output_aliases={2: 0},
        compiler_params=PARAMS,
        cost_estimate=pl.CostEstimate(flops=1 << 30, bytes_accessed=1 << 20, transcendentals=0),
        name="first_sums",
    )(*sources, own)
    selector, band, scale = pl.pallas_call(
        ready_kernel,
        out_shape=[
            jax.ShapeDtypeStruct((Q2 * trials, R2 * nsub), jnp.bfloat16),
            jax.ShapeDtypeStruct((LANES + WMAX, count * LANES), jnp.bfloat16),
            jax.ShapeDtypeStruct((count, LANES), jnp.float32),
        ],
        in_specs=[HBM] * 2,
        out_specs=[VMEM] * 3,
        scratch_shapes=[
            pltpu.VMEM(fine.shape, fine.dtype),
            pltpu.SMEM(widths.shape, widths.dtype),
            pltpu.SemaphoreType.DMA((2,)),
        ],
        compiler_params=PARAMS,
        cost_estimate=pl.CostEstimate(flops=1 << 30, bytes_accessed=1 << 20, transcendentals=0),
        name="ready",
    )(*(pltpu.with_memory_space_constraint(x, pltpu.HBM) for x in (fine, widths)))
    subbands = pl.pallas_call(
        join_kernel,
        out_shape=jax.ShapeDtypeStruct((nblk * CHUNKS, LANES), jnp.bfloat16),
        in_specs=[VMEM] * 3,
        out_specs=VMEM,
        scratch_shapes=[pltpu.VMEM((nblk * CHUNKS, LANES), jnp.float32)],
        compiler_params=PARAMS,
        name="join",
    )(own, following, scale)
    received = lax.all_to_all(
        subbands,
        "chan",
        split_axis=0,
        concat_axis=0,
        tiled=True,
        axis_index_groups=[[listed(i, groups) for i in range(groups)]],
    )
    return pl.pallas_call(
        trial_kernel,
        out_shape=jax.ShapeDtypeStruct((count, trials, steps), jnp.bfloat16),
        in_specs=[VMEM] * 4,
        out_specs=VMEM,
        scratch_shapes=[pltpu.VMEM((nsub * CHUNKS, LANES), jnp.float32)],
        compiler_params=PARAMS,
        name="trials",
    )(received, selector, band, scale)


def solution(mesh):
    return jax.shard_map(
        per_device,
        mesh=mesh,
        in_specs=(P("chan", "tm"), P("chan", None), P(None, "chan", None), P()),
        out_specs=P(None, "chan", "tm"),
        check_vma=False,
    )
```

```python
import functools
import math

import jax
import jax.numpy as jnp
from jax import lax
from jax.experimental import pallas as pl
from jax.experimental.pallas import tpu as pltpu
from jax.sharding import PartitionSpec as P

CHANNELS = 16384
D1MAX = 95
D2MAX = 31
WMAX = 128
LANES = 128
MARGIN = D1MAX + 1
R1 = 16
Q1 = (D1MAX + 1) // R1
R2 = 4
Q2 = (D2MAX + 1) // R2
BASE = 42
CHUNKS = 4


def shift_left(x, by):
    if by == 0:
        return x
    return jnp.concatenate([x[:, by:], jnp.zeros((x.shape[0], by), x.dtype)], axis=1)


def turn_left(x, by):
    if by == 0:
        return x
    return jnp.concatenate([x[:, by:], x[:, :by]], axis=1)


def listed(i, count):
    return (i + BASE) % count ^ 1


def in_listed_order(x):
    count = x.shape[0]
    x = jnp.concatenate([x[BASE:], x[:BASE]], axis=0)
    even = lax.broadcasted_iota(jnp.int32, x.shape, 0) % 2 == 0
    return jnp.where(even, pltpu.roll(x, count - 1, 0), pltpu.roll(x, 1, 0))


def one_hot(delay, level):
    return jnp.where(delay == level, jnp.ones((), jnp.bfloat16), jnp.zeros((), jnp.bfloat16))


def own_sums(
    spectra_hbm, delay_hbm, out_ref, sent_ref,
    spectra_ref, delay_ref, acc_ref, before_ref, sems,
):
    copies = [
        pltpu.make_async_copy(spectra_hbm, spectra_ref, sems.at[0]),
        pltpu.make_async_copy(delay_hbm, delay_ref, sems.at[1]),
    ]
    for copy in copies:
        copy.start()
    for copy in copies:
        copy.wait()
    nblk, steps = out_ref.shape
    last = steps - LANES
    spectra = spectra_ref[...]
    delay = in_listed_order(delay_ref[...]).astype(jnp.bfloat16)
    lane = lax.broadcasted_iota(jnp.int32, (1, LANES), 1)
    for r in range(R1):
        selector = jnp.concatenate([one_hot(delay, float(R1 * q + r)) for q in range(Q1)], axis=0)
        part = jnp.dot(selector, turn_left(spectra, r), preferred_element_type=jnp.float32)
        if r == 0:
            acc_ref[...] = part
            continue
        acc_ref[...] += part
        over = jnp.where(lane >= LANES - r, part[:, last:], 0.0)
        if r == 1:
            before_ref[...] = over
        else:
            before_ref[...] += over
    total = jnp.zeros((nblk, LANES + steps), jnp.float32)
    for q in range(Q1):
        rows = slice(nblk * q, nblk * (q + 1))
        over = before_ref[rows, :]
        total = total + shift_left(
            jnp.concatenate([over, acc_ref[rows, :last], acc_ref[rows, last:] - over], axis=1),
            R1 * q,
        )
    out_ref[...] = total[:, LANES:]
    if sent_ref is not None:
        around = jnp.where(lane < LANES - MARGIN, total[:, 2 * LANES :], total[:, :LANES])
        sent_ref[...] = jnp.concatenate([total[:, LANES : 2 * LANES], around], axis=1).astype(
            jnp.bfloat16
        )


def sender_kernel(spectra_hbm, delay_hbm, out_ref, sent_ref, *scratch):
    @pl.when(lax.axis_index("tm") > 0)
    def _():
        own_sums(spectra_hbm, delay_hbm, out_ref, sent_ref, *scratch)


def first_kernel(spectra_hbm, delay_hbm, sums_ref, out_ref, *scratch):
    del sums_ref

    @pl.when(lax.axis_index("tm") == 0)
    def _():
        own_sums(spectra_hbm, delay_hbm, out_ref, None, *scratch)


def ready_kernel(fine_hbm, widths_hbm, selector_ref, band_ref, scale_ref, fine_ref, widths_ref, sems):
    copies = [
        pltpu.make_async_copy(fine_hbm, fine_ref, sems.at[0]),
        pltpu.make_async_copy(widths_hbm, widths_ref, sems.at[1]),
    ]
    for copy in copies:
        copy.start()
    for copy in copies:
        copy.wait()
    nsub = fine_ref.shape[1]
    subband = lax.broadcasted_iota(jnp.int32, (nsub, nsub), 0)
    place = lax.broadcasted_iota(jnp.int32, (nsub, nsub), 1)
    place = 2 * (place % (nsub // 2)) + place // (nsub // 2)
    order = jnp.where(subband == listed(place, nsub), 1.0, 0.0).astype(jnp.bfloat16)
    fine = jnp.dot(fine_ref[...].astype(jnp.bfloat16), order, preferred_element_type=jnp.float32)
    fine = jnp.concatenate([fine - r for r in range(R2)], axis=1).astype(jnp.bfloat16)
    selector_ref[...] = jnp.concatenate([one_hot(fine, float(R2 * q)) for q in range(Q2)], axis=0)
    shape = (band_ref.shape[0], LANES)
    ahead = lax.broadcasted_iota(jnp.int32, shape, 0) - lax.broadcasted_iota(jnp.int32, shape, 1)
    for index in range(scale_ref.shape[0]):
        width = widths_ref[index]
        counts = jnp.logical_and(ahead >= 0, ahead < width)
        band_ref[:, LANES * index : LANES * (index + 1)] = jnp.where(counts, 1.0, 0.0).astype(jnp.bfloat16)
        scale_ref[index : index + 1, :] = (1.0 / math.sqrt(CHANNELS)) / jnp.sqrt(
            jnp.full((1, LANES), width).astype(jnp.float32)
        )


def join_kernel(own_ref, next_ref, ready_ref, out_ref, rows_ref):
    del ready_ref
    nblk = own_ref.shape[0]
    following = next_ref[...].astype(jnp.float32)
    chunks = [own_ref[:, :LANES], own_ref[:, LANES:], following[:, :LANES], following[:, LANES:]]
    for m, chunk in enumerate(chunks):
        rows_ref[pl.ds(m, nblk, stride=CHUNKS), :] = chunk
    out_ref[...] = rows_ref[...].astype(jnp.bfloat16)


def trial_kernel(sub_ref, selector_ref, band_ref, scale_ref, out_ref, rows_ref):
    count, trials, steps = out_ref.shape
    nsub = sub_ref.shape[0] // CHUNKS
    rows_ref[...] = sub_ref[...].astype(jnp.float32)

    def chunk(m, first, second):
        return jnp.concatenate(
            [rows_ref[pl.ds(CHUNKS * odd + m, nsub // 2, stride=2 * CHUNKS), :] for odd in (first, second)],
            axis=0,
        )

    around = chunk(3, 1, 0)
    lane = lax.broadcasted_iota(jnp.int32, around.shape, 1)
    sub = jnp.concatenate(
        [
            chunk(0, 0, 1),
            chunk(1, 0, 1) + jnp.where(lane < LANES - MARGIN, 0.0, around),
            chunk(2, 1, 0),
            around,
        ],
        axis=1,
    )
    shifted = jnp.concatenate(
        [turn_left(sub, r).astype(jnp.bfloat16) for r in range(R2)], axis=0
    )
    parts = jnp.dot(selector_ref[...], shifted, preferred_element_type=jnp.float32)
    series = parts[:trials]
    for q in range(1, Q2):
        series = series + shift_left(parts[trials * q : trials * (q + 1)], R2 * q)
    series = series[:, : steps + WMAX]
    high = series.astype(jnp.bfloat16)
    terms = (high, (series - high.astype(jnp.float32)).astype(jnp.bfloat16))
    reach = band_ref.shape[0]
    halves = range(0, steps, LANES)
    windows = jnp.concatenate([term[:, t : t + reach] for t in halves for term in terms], axis=0)
    sums = jnp.dot(windows, band_ref[...], preferred_element_type=jnp.float32)
    sums = sums.reshape(len(halves), len(terms), trials, count * LANES)
    for index in range(count):
        columns = slice(LANES * index, LANES * (index + 1))
        scale = scale_ref[index : index + 1, :]
        for half, t in enumerate(halves):
            first, second = (sums[half, term, :, columns] for term in range(len(terms)))
            out_ref[index, :, t : t + LANES] = ((first + second) * scale).astype(jnp.bfloat16)


VMEM = pl.BlockSpec(memory_space=pltpu.VMEM)
HBM = pl.BlockSpec(memory_space=pltpu.HBM)
PARAMS = pltpu.CompilerParams(vmem_limit_bytes=16 * 1024 * 1024)


def per_device(spectra, coarse_delay, fine_delay, widths):
    channels, steps = spectra.shape
    nblk = coarse_delay.shape[1]
    nsub, _, trials = fine_delay.shape
    count = widths.shape[0]
    by_block = coarse_delay.T
    fine = fine_delay.reshape(nsub, trials).T
    block = jax.ShapeDtypeStruct((nblk, steps), jnp.float32)
    scratch = [
        pltpu.VMEM(spectra.shape, spectra.dtype),
        pltpu.VMEM(by_block.shape, by_block.dtype),
        pltpu.VMEM((Q1 * nblk, steps), jnp.float32),
        pltpu.VMEM((Q1 * nblk, LANES), jnp.float32),
        pltpu.SemaphoreType.DMA((2,)),
    ]
    sources = [pltpu.with_memory_space_constraint(x, pltpu.HBM) for x in (spectra, by_block)]
    own, sent = pl.pallas_call(
        sender_kernel,
        out_shape=[block, jax.ShapeDtypeStruct((nblk, steps), jnp.bfloat16)],
        in_specs=[HBM] * 2,
        out_specs=[VMEM] * 2,
        scratch_shapes=scratch,
        compiler_params=PARAMS,
        name="sender_sums",
    )(*sources)
    blocks = lax.axis_size("tm")
    groups = lax.axis_size("chan")
    following = lax.ppermute(
        sent,
        ("chan", "tm"),
        [
            (c * blocks + z + 1, (c ^ 1) * blocks + z)
            for c in range(groups)
            for z in range(blocks - 1)
        ],
    )
    own = pl.pallas_call(
        first_kernel,
        out_shape=block,
        in_specs=[HBM] * 2 + [VMEM],
        out_specs=VMEM,
        scratch_shapes=scratch,
        input_output_aliases={2: 0},
        compiler_params=PARAMS,
        cost_estimate=pl.CostEstimate(flops=1 << 30, bytes_accessed=1 << 20, transcendentals=0),
        name="first_sums",
    )(*sources, own)
    selector, band, scale = pl.pallas_call(
        ready_kernel,
        out_shape=[
            jax.ShapeDtypeStruct((Q2 * trials, R2 * nsub), jnp.bfloat16),
            jax.ShapeDtypeStruct((LANES + WMAX, count * LANES), jnp.bfloat16),
            jax.ShapeDtypeStruct((count, LANES), jnp.float32),
        ],
        in_specs=[HBM] * 2,
        out_specs=[VMEM] * 3,
        scratch_shapes=[
            pltpu.VMEM(fine.shape, fine.dtype),
            pltpu.SMEM(widths.shape, widths.dtype),
            pltpu.SemaphoreType.DMA((2,)),
        ],
        compiler_params=PARAMS,
        cost_estimate=pl.CostEstimate(flops=1 << 30, bytes_accessed=1 << 20, transcendentals=0),
        name="ready",
    )(*(pltpu.with_memory_space_constraint(x, pltpu.HBM) for x in (fine, widths)))
    subbands = pl.pallas_call(
        join_kernel,
        out_shape=jax.ShapeDtypeStruct((nblk * CHUNKS, LANES), jnp.bfloat16),
        in_specs=[VMEM] * 3,
        out_specs=VMEM,
        scratch_shapes=[pltpu.VMEM((nblk * CHUNKS, LANES), jnp.float32)],
        compiler_params=PARAMS,
        name="join",
    )(own, following, scale)
    received = lax.all_to_all(
        subbands,
        "chan",
        split_axis=0,
        concat_axis=0,
        tiled=True,
        axis_index_groups=[[listed(i, groups) for i in range(groups)]],
    )
    return pl.pallas_call(
        trial_kernel,
        out_shape=jax.ShapeDtypeStruct((count, trials, steps), jnp.bfloat16),
        in_specs=[VMEM] * 4,
        out_specs=VMEM,
        scratch_shapes=[pltpu.VMEM((nsub * CHUNKS, LANES), jnp.float32)],
        compiler_params=PARAMS,
        name="trials",
    )(received, selector, band, scale)


def solution(mesh):
    return jax.shard_map(
        per_device,
        mesh=mesh,
        in_specs=(P("chan", "tm"), P("chan", None), P(None, "chan", None), P()),
        out_specs=P(None, "chan", "tm"),
        check_vma=False,
    )
```

```python
import functools
import math

import jax
import jax.numpy as jnp
from jax import lax
from jax.experimental import pallas as pl
from jax.experimental.pallas import tpu as pltpu
from jax.sharding import PartitionSpec as P

CHANNELS = 16384
D1MAX = 95
D2MAX = 31
WMAX = 128
LANES = 128
MARGIN = D1MAX + 1
R1 = 16
Q1 = (D1MAX + 1) // R1
R2 = 4
Q2 = (D2MAX + 1) // R2
BASE = 42
CHUNKS = 4


def shift_left(x, by):
    if by == 0:
        return x
    return jnp.concatenate([x[:, by:], jnp.zeros((x.shape[0], by), x.dtype)], axis=1)


def turn_left(x, by):
    if by == 0:
        return x
    return jnp.concatenate([x[:, by:], x[:, :by]], axis=1)


def listed(i, count):
    return (i + BASE) % count ^ 1


def in_listed_order(x):
    count = x.shape[0]
    x = jnp.concatenate([x[BASE:], x[:BASE]], axis=0)
    even = lax.broadcasted_iota(jnp.int32, x.shape, 0) % 2 == 0
    return jnp.where(even, pltpu.roll(x, count - 1, 0), pltpu.roll(x, 1, 0))


def one_hot(delay, level):
    return jnp.where(delay == level, jnp.ones((), jnp.bfloat16), jnp.zeros((), jnp.bfloat16))


def own_sums(
    spectra_hbm, delay_hbm, out_ref, sent_ref,
    spectra_ref, delay_ref, acc_ref, before_ref, sems,
):
    copies = [
        pltpu.make_async_copy(spectra_hbm, spectra_ref, sems.at[0]),
        pltpu.make_async_copy(delay_hbm, delay_ref, sems.at[1]),
    ]
    for copy in copies:
        copy.start()
    for copy in copies:
        copy.wait()
    nblk, steps = out_ref.shape
    last = steps - LANES
    spectra = spectra_ref[...]
    delay = in_listed_order(delay_ref[...]).astype(jnp.bfloat16)
    lane = lax.broadcasted_iota(jnp.int32, (1, LANES), 1)
    for r in range(R1):
        selector = jnp.concatenate([one_hot(delay, float(R1 * q + r)) for q in range(Q1)], axis=0)
        part = jnp.dot(selector, turn_left(spectra, r), preferred_element_type=jnp.float32)
        if r == 0:
            acc_ref[...] = part
            continue
        acc_ref[...] += part
        over = jnp.where(lane >= LANES - r, part[:, last:], 0.0)
        if r == 1:
            before_ref[...] = over
        else:
            before_ref[...] += over
    total = jnp.zeros((nblk, LANES + steps), jnp.float32)
    for q in range(Q1):
        rows = slice(nblk * q, nblk * (q + 1))
        over = before_ref[rows, :]
        total = total + shift_left(
            jnp.concatenate([over, acc_ref[rows, :last], acc_ref[rows, last:] - over], axis=1),
            R1 * q,
        )
    out_ref[...] = total[:, LANES:]
    if sent_ref is not None:
        around = jnp.where(lane < LANES - MARGIN, total[:, 2 * LANES :], total[:, :LANES])
        sent_ref[...] = jnp.concatenate([total[:, LANES : 2 * LANES], around], axis=1).astype(
            jnp.bfloat16
        )


def sender_kernel(spectra_hbm, delay_hbm, out_ref, sent_ref, *scratch):
    @pl.when(lax.axis_index("tm") > 0)
    def _():
        own_sums(spectra_hbm, delay_hbm, out_ref, sent_ref, *scratch)


def beside_kernel(
    spectra_hbm, delay_hbm, sums_ref, fine_hbm, widths_hbm,
    out_ref, selector_ref, band_ref, scale_ref,
    fine_ref, widths_ref, load_sems, *scratch,
):
    del sums_ref
    copies = [
        pltpu.make_async_copy(fine_hbm, fine_ref, load_sems.at[0]),
        pltpu.make_async_copy(widths_hbm, widths_ref, load_sems.at[1]),
    ]
    for copy in copies:
        copy.start()

    @pl.when(lax.axis_index("tm") == 0)
    def _():
        own_sums(spectra_hbm, delay_hbm, out_ref, None, *scratch)

    for copy in copies:
        copy.wait()
    nsub = fine_ref.shape[1]
    subband = lax.broadcasted_iota(jnp.int32, (nsub, nsub), 0)
    place = lax.broadcasted_iota(jnp.int32, (nsub, nsub), 1)
    place = 2 * (place % (nsub // 2)) + place // (nsub // 2)
    order = jnp.where(subband == listed(place, nsub), 1.0, 0.0).astype(jnp.bfloat16)
    fine = jnp.dot(fine_ref[...].astype(jnp.bfloat16), order, preferred_element_type=jnp.float32)
    fine = jnp.concatenate([fine - r for r in range(R2)], axis=1).astype(jnp.bfloat16)
    selector_ref[...] = jnp.concatenate([one_hot(fine, float(R2 * q)) for q in range(Q2)], axis=0)
    shape = (band_ref.shape[0], LANES)
    ahead = lax.broadcasted_iota(jnp.int32, shape, 0) - lax.broadcasted_iota(jnp.int32, shape, 1)
    for index in range(scale_ref.shape[0]):
        width = widths_ref[index]
        counts = jnp.logical_and(ahead >= 0, ahead < width)
        band_ref[:, LANES * index : LANES * (index + 1)] = jnp.where(counts, 1.0, 0.0).astype(jnp.bfloat16)
        scale_ref[index : index + 1, :] = (1.0 / math.sqrt(CHANNELS)) / jnp.sqrt(
            jnp.full((1, LANES), width).astype(jnp.float32)
        )


def join_kernel(own_ref, next_ref, out_ref, rows_ref):
    nblk = own_ref.shape[0]
    following = next_ref[...].astype(jnp.float32)
    chunks = [own_ref[:, :LANES], own_ref[:, LANES:], following[:, :LANES], following[:, LANES:]]
    for m, chunk in enumerate(chunks):
        rows_ref[pl.ds(m, nblk, stride=CHUNKS), :] = chunk
    out_ref[...] = rows_ref[...].astype(jnp.bfloat16)


def trial_kernel(sub_ref, selector_ref, band_ref, scale_ref, out_ref, rows_ref):
    count, trials, steps = out_ref.shape
    nsub = sub_ref.shape[0] // CHUNKS
    rows_ref[...] = sub_ref[...].astype(jnp.float32)

    def chunk(m, first, second):
        return jnp.concatenate(
            [rows_ref[pl.ds(CHUNKS * odd + m, nsub // 2, stride=2 * CHUNKS), :] for odd in (first, second)],
            axis=0,
        )

    around = chunk(3, 1, 0)
    lane = lax.broadcasted_iota(jnp.int32, around.shape, 1)
    sub = jnp.concatenate(
        [
            chunk(0, 0, 1),
            chunk(1, 0, 1) + jnp.where(lane < LANES - MARGIN, 0.0, around),
            chunk(2, 1, 0),
            around,
        ],
        axis=1,
    )
    shifted = jnp.concatenate(
        [turn_left(sub, r).astype(jnp.bfloat16) for r in range(R2)], axis=0
    )
    parts = jnp.dot(selector_ref[...], shifted, preferred_element_type=jnp.float32)
    series = parts[:trials]
    for q in range(1, Q2):
        series = series + shift_left(parts[trials * q : trials * (q + 1)], R2 * q)
    series = series[:, : steps + WMAX]
    high = series.astype(jnp.bfloat16)
    terms = (high, (series - high.astype(jnp.float32)).astype(jnp.bfloat16))
    reach = band_ref.shape[0]
    halves = range(0, steps, LANES)
    windows = jnp.concatenate([term[:, t : t + reach] for t in halves for term in terms], axis=0)
    sums = jnp.dot(windows, band_ref[...], preferred_element_type=jnp.float32)
    sums = sums.reshape(len(halves), len(terms), trials, count * LANES)
    for index in range(count):
        columns = slice(LANES * index, LANES * (index + 1))
        scale = scale_ref[index : index + 1, :]
        for half, t in enumerate(halves):
            first, second = (sums[half, term, :, columns] for term in range(len(terms)))
            out_ref[index, :, t : t + LANES] = ((first + second) * scale).astype(jnp.bfloat16)


VMEM = pl.BlockSpec(memory_space=pltpu.VMEM)
HBM = pl.BlockSpec(memory_space=pltpu.HBM)
PARAMS = pltpu.CompilerParams(vmem_limit_bytes=16 * 1024 * 1024)


def per_device(spectra, coarse_delay, fine_delay, widths):
    channels, steps = spectra.shape
    nblk = coarse_delay.shape[1]
    nsub, _, trials = fine_delay.shape
    count = widths.shape[0]
    by_block = coarse_delay.T
    fine = fine_delay.reshape(nsub, trials).T
    block = jax.ShapeDtypeStruct((nblk, steps), jnp.float32)
    scratch = [
        pltpu.VMEM(spectra.shape, spectra.dtype),
        pltpu.VMEM(by_block.shape, by_block.dtype),
        pltpu.VMEM((Q1 * nblk, steps), jnp.float32),
        pltpu.VMEM((Q1 * nblk, LANES), jnp.float32),
        pltpu.SemaphoreType.DMA((2,)),
    ]
    sources = [pltpu.with_memory_space_constraint(x, pltpu.HBM) for x in (spectra, by_block)]
    own, sent = pl.pallas_call(
        sender_kernel,
        out_shape=[block, jax.ShapeDtypeStruct((nblk, steps), jnp.bfloat16)],
        in_specs=[HBM] * 2,
        out_specs=[VMEM] * 2,
        scratch_shapes=scratch,
        compiler_params=PARAMS,
        name="sender_sums",
    )(*sources)
    blocks = lax.axis_size("tm")
    groups = lax.axis_size("chan")
    following = lax.ppermute(
        sent,
        ("chan", "tm"),
        [
            (c * blocks + z + 1, (c ^ 1) * blocks + z)
            for c in range(groups)
            for z in range(blocks - 1)
        ],
    )
    own, selector, band, scale = pl.pallas_call(
        beside_kernel,
        out_shape=[
            block,
            jax.ShapeDtypeStruct((Q2 * trials, R2 * nsub), jnp.bfloat16),
            jax.ShapeDtypeStruct((LANES + WMAX, count * LANES), jnp.bfloat16),
            jax.ShapeDtypeStruct((count, LANES), jnp.float32),
        ],
        in_specs=[HBM] * 2 + [VMEM] + [HBM] * 2,
        out_specs=[VMEM] * 4,
        scratch_shapes=[
            pltpu.VMEM(fine.shape, fine.dtype),
            pltpu.SMEM(widths.shape, widths.dtype),
            pltpu.SemaphoreType.DMA((2,)),
            *scratch,
        ],
        input_output_aliases={2: 0},
        compiler_params=PARAMS,
        cost_estimate=pl.CostEstimate(flops=1 << 30, bytes_accessed=1 << 20, transcendentals=0),
        name="beside",
    )(*sources, own, *(pltpu.with_memory_space_constraint(x, pltpu.HBM) for x in (fine, widths)))
    subbands = pl.pallas_call(
        join_kernel,
        out_shape=jax.ShapeDtypeStruct((nblk * CHUNKS, LANES), jnp.bfloat16),
        in_specs=[VMEM] * 2,
        out_specs=VMEM,
        scratch_shapes=[pltpu.VMEM((nblk * CHUNKS, LANES), jnp.float32)],
        compiler_params=PARAMS,
        name="join",
    )(own, following)
    received = lax.all_to_all(
        subbands,
        "chan",
        split_axis=0,
        concat_axis=0,
        tiled=True,
        axis_index_groups=[[listed(i, groups) for i in range(groups)]],
    )
    return pl.pallas_call(
        trial_kernel,
        out_shape=jax.ShapeDtypeStruct((count, trials, steps), jnp.bfloat16),
        in_specs=[VMEM] * 4,
        out_specs=VMEM,
        scratch_shapes=[pltpu.VMEM((nsub * CHUNKS, LANES), jnp.float32)],
        compiler_params=PARAMS,
        name="trials",
    )(received, selector, band, scale)


def solution(mesh):
    return jax.shard_map(
        per_device,
        mesh=mesh,
        in_specs=(P("chan", "tm"), P("chan", None), P(None, "chan", None), P()),
        out_specs=P(None, "chan", "tm"),
        check_vma=False,
    )
```

```python
import functools
import math

import jax
import jax.numpy as jnp
from jax import lax
from jax.experimental import pallas as pl
from jax.experimental.pallas import tpu as pltpu
from jax.sharding import PartitionSpec as P

CHANNELS = 16384
D1MAX = 95
D2MAX = 31
WMAX = 128
LANES = 128
MARGIN = D1MAX + 1
R1 = 16
Q1 = (D1MAX + 1) // R1
R2 = 4
Q2 = (D2MAX + 1) // R2
BASE = 42
CHUNKS = 4


def shift_left(x, by):
    if by == 0:
        return x
    return jnp.concatenate([x[:, by:], jnp.zeros((x.shape[0], by), x.dtype)], axis=1)


def turn_left(x, by):
    if by == 0:
        return x
    return jnp.concatenate([x[:, by:], x[:, :by]], axis=1)


def listed(i, count):
    return (i + BASE) % count ^ 1


def in_listed_order(x):
    count = x.shape[0]
    x = jnp.concatenate([x[BASE:], x[:BASE]], axis=0)
    even = lax.broadcasted_iota(jnp.int32, x.shape, 0) % 2 == 0
    return jnp.where(even, pltpu.roll(x, count - 1, 0), pltpu.roll(x, 1, 0))


def one_hot(delay, level):
    return jnp.where(delay == level, jnp.ones((), jnp.bfloat16), jnp.zeros((), jnp.bfloat16))


def own_sums(
    spectra_hbm, delay_hbm, out_ref, sent_ref,
    spectra_ref, delay_ref, acc_ref, before_ref, sems,
):
    half = spectra_ref.shape[0] // 2
    copies = [pltpu.make_async_copy(delay_hbm, delay_ref, sems.at[0])] + [
        pltpu.make_async_copy(
            spectra_hbm.at[pl.ds(half * i, half)], spectra_ref.at[pl.ds(half * i, half)], sems.at[i + 1]
        )
        for i in range(2)
    ]
    for copy in copies:
        copy.start()
    for copy in copies:
        copy.wait()
    nblk, steps = out_ref.shape
    last = steps - LANES
    spectra = spectra_ref[...]
    delay = in_listed_order(delay_ref[...]).astype(jnp.bfloat16)
    lane = lax.broadcasted_iota(jnp.int32, (1, LANES), 1)
    for r in range(R1):
        selector = jnp.concatenate([one_hot(delay, float(R1 * q + r)) for q in range(Q1)], axis=0)
        part = jnp.dot(selector, turn_left(spectra, r), preferred_element_type=jnp.float32)
        if r == 0:
            acc_ref[...] = part
            continue
        acc_ref[...] += part
        over = jnp.where(lane >= LANES - r, part[:, last:], 0.0)
        if r == 1:
            before_ref[...] = over
        else:
            before_ref[...] += over
    total = jnp.zeros((nblk, LANES + steps), jnp.float32)
    for q in range(Q1):
        rows = slice(nblk * q, nblk * (q + 1))
        over = before_ref[rows, :]
        total = total + shift_left(
            jnp.concatenate([over, acc_ref[rows, :last], acc_ref[rows, last:] - over], axis=1),
            R1 * q,
        )
    out_ref[...] = total[:, LANES:]
    if sent_ref is not None:
        around = jnp.where(lane < LANES - MARGIN, total[:, 2 * LANES :], total[:, :LANES])
        sent_ref[...] = jnp.concatenate([total[:, LANES : 2 * LANES], around], axis=1).astype(
            jnp.bfloat16
        )


def sender_kernel(spectra_hbm, delay_hbm, out_ref, sent_ref, *scratch):
    @pl.when(lax.axis_index("tm") > 0)
    def _():
        own_sums(spectra_hbm, delay_hbm, out_ref, sent_ref, *scratch)


def beside_kernel(
    spectra_hbm, delay_hbm, sums_ref, fine_hbm, widths_hbm,
    out_ref, selector_ref, band_ref, scale_ref,
    fine_ref, widths_ref, load_sems, *scratch,
):
    del sums_ref
    copies = [
        pltpu.make_async_copy(fine_hbm, fine_ref, load_sems.at[0]),
        pltpu.make_async_copy(widths_hbm, widths_ref, load_sems.at[1]),
    ]
    for copy in copies:
        copy.start()

    @pl.when(lax.axis_index("tm") == 0)
    def _():
        own_sums(spectra_hbm, delay_hbm, out_ref, None, *scratch)

    for copy in copies:
        copy.wait()
    nsub = fine_ref.shape[1]
    subband = lax.broadcasted_iota(jnp.int32, (nsub, nsub), 0)
    place = lax.broadcasted_iota(jnp.int32, (nsub, nsub), 1)
    place = 2 * (place % (nsub // 2)) + place // (nsub // 2)
    order = jnp.where(subband == listed(place, nsub), 1.0, 0.0).astype(jnp.bfloat16)
    fine = jnp.dot(fine_ref[...].astype(jnp.bfloat16), order, preferred_element_type=jnp.float32)
    fine = jnp.concatenate([fine - r for r in range(R2)], axis=1).astype(jnp.bfloat16)
    selector_ref[...] = jnp.concatenate([one_hot(fine, float(R2 * q)) for q in range(Q2)], axis=0)
    shape = (band_ref.shape[0], LANES)
    ahead = lax.broadcasted_iota(jnp.int32, shape, 0) - lax.broadcasted_iota(jnp.int32, shape, 1)
    for index in range(scale_ref.shape[0]):
        width = widths_ref[index]
        counts = jnp.logical_and(ahead >= 0, ahead < width)
        band_ref[:, LANES * index : LANES * (index + 1)] = jnp.where(counts, 1.0, 0.0).astype(jnp.bfloat16)
        scale_ref[index : index + 1, :] = (1.0 / math.sqrt(CHANNELS)) / jnp.sqrt(
            jnp.full((1, LANES), width).astype(jnp.float32)
        )


def join_kernel(own_ref, next_ref, out_ref, rows_ref):
    nblk = own_ref.shape[0]
    following = next_ref[...].astype(jnp.float32)
    chunks = [own_ref[:, :LANES], own_ref[:, LANES:], following[:, :LANES], following[:, LANES:]]
    for m, chunk in enumerate(chunks):
        rows_ref[pl.ds(m, nblk, stride=CHUNKS), :] = chunk
    out_ref[...] = rows_ref[...].astype(jnp.bfloat16)


def trial_kernel(sub_ref, selector_ref, band_ref, scale_ref, out_ref, rows_ref):
    count, trials, steps = out_ref.shape
    nsub = sub_ref.shape[0] // CHUNKS
    rows_ref[...] = sub_ref[...].astype(jnp.float32)

    def chunk(m, first, second):
        return jnp.concatenate(
            [rows_ref[pl.ds(CHUNKS * odd + m, nsub // 2, stride=2 * CHUNKS), :] for odd in (first, second)],
            axis=0,
        )

    around = chunk(3, 1, 0)
    lane = lax.broadcasted_iota(jnp.int32, around.shape, 1)
    sub = jnp.concatenate(
        [
            chunk(0, 0, 1),
            chunk(1, 0, 1) + jnp.where(lane < LANES - MARGIN, 0.0, around),
            chunk(2, 1, 0),
            around,
        ],
        axis=1,
    )
    shifted = jnp.concatenate(
        [turn_left(sub, r).astype(jnp.bfloat16) for r in range(R2)], axis=0
    )
    parts = jnp.dot(selector_ref[...], shifted, preferred_element_type=jnp.float32)
    series = parts[:trials]
    for q in range(1, Q2):
        series = series + shift_left(parts[trials * q : trials * (q + 1)], R2 * q)
    series = series[:, : steps + WMAX]
    high = series.astype(jnp.bfloat16)
    terms = (high, (series - high.astype(jnp.float32)).astype(jnp.bfloat16))
    reach = band_ref.shape[0]
    halves = range(0, steps, LANES)
    windows = jnp.concatenate([term[:, t : t + reach] for t in halves for term in terms], axis=0)
    sums = jnp.dot(windows, band_ref[...], preferred_element_type=jnp.float32)
    sums = sums.reshape(len(halves), len(terms), trials, count * LANES)
    for index in range(count):
        columns = slice(LANES * index, LANES * (index + 1))
        scale = scale_ref[index : index + 1, :]
        for half, t in enumerate(halves):
            first, second = (sums[half, term, :, columns] for term in range(len(terms)))
            out_ref[index, :, t : t + LANES] = ((first + second) * scale).astype(jnp.bfloat16)


VMEM = pl.BlockSpec(memory_space=pltpu.VMEM)
HBM = pl.BlockSpec(memory_space=pltpu.HBM)
PARAMS = pltpu.CompilerParams(vmem_limit_bytes=16 * 1024 * 1024)


def per_device(spectra, coarse_delay, fine_delay, widths):
    channels, steps = spectra.shape
    nblk = coarse_delay.shape[1]
    nsub, _, trials = fine_delay.shape
    count = widths.shape[0]
    by_block = coarse_delay.T
    fine = fine_delay.reshape(nsub, trials).T
    block = jax.ShapeDtypeStruct((nblk, steps), jnp.float32)
    scratch = [
        pltpu.VMEM(spectra.shape, spectra.dtype),
        pltpu.VMEM(by_block.shape, by_block.dtype),
        pltpu.VMEM((Q1 * nblk, steps), jnp.float32),
        pltpu.VMEM((Q1 * nblk, LANES), jnp.float32),
        pltpu.SemaphoreType.DMA((3,)),
    ]
    sources = [pltpu.with_memory_space_constraint(x, pltpu.HBM) for x in (spectra, by_block)]
    own, sent = pl.pallas_call(
        sender_kernel,
        out_shape=[block, jax.ShapeDtypeStruct((nblk, steps), jnp.bfloat16)],
        in_specs=[HBM] * 2,
        out_specs=[VMEM] * 2,
        scratch_shapes=scratch,
        compiler_params=PARAMS,
        name="sender_sums",
    )(*sources)
    blocks = lax.axis_size("tm")
    groups = lax.axis_size("chan")
    following = lax.ppermute(
        sent,
        ("chan", "tm"),
        [
            (c * blocks + z + 1, (c ^ 1) * blocks + z)
            for c in range(groups)
            for z in range(blocks - 1)
        ],
    )
    own, selector, band, scale = pl.pallas_call(
        beside_kernel,
        out_shape=[
            block,
            jax.ShapeDtypeStruct((Q2 * trials, R2 * nsub), jnp.bfloat16),
            jax.ShapeDtypeStruct((LANES + WMAX, count * LANES), jnp.bfloat16),
            jax.ShapeDtypeStruct((count, LANES), jnp.float32),
        ],
        in_specs=[HBM] * 2 + [VMEM] + [HBM] * 2,
        out_specs=[VMEM] * 4,
        scratch_shapes=[
            pltpu.VMEM(fine.shape, fine.dtype),
            pltpu.SMEM(widths.shape, widths.dtype),
            pltpu.SemaphoreType.DMA((2,)),
            *scratch,
        ],
        input_output_aliases={2: 0},
        compiler_params=PARAMS,
        cost_estimate=pl.CostEstimate(flops=1 << 30, bytes_accessed=1 << 20, transcendentals=0),
        name="beside",
    )(*sources, own, *(pltpu.with_memory_space_constraint(x, pltpu.HBM) for x in (fine, widths)))
    subbands = pl.pallas_call(
        join_kernel,
        out_shape=jax.ShapeDtypeStruct((nblk * CHUNKS, LANES), jnp.bfloat16),
        in_specs=[VMEM] * 2,
        out_specs=VMEM,
        scratch_shapes=[pltpu.VMEM((nblk * CHUNKS, LANES), jnp.float32)],
        compiler_params=PARAMS,
        name="join",
    )(own, following)
    received = lax.all_to_all(
        subbands,
        "chan",
        split_axis=0,
        concat_axis=0,
        tiled=True,
        axis_index_groups=[[listed(i, groups) for i in range(groups)]],
    )
    return pl.pallas_call(
        trial_kernel,
        out_shape=jax.ShapeDtypeStruct((count, trials, steps), jnp.bfloat16),
        in_specs=[VMEM] * 4,
        out_specs=VMEM,
        scratch_shapes=[pltpu.VMEM((nsub * CHUNKS, LANES), jnp.float32)],
        compiler_params=PARAMS,
        name="trials",
    )(received, selector, band, scale)


def solution(mesh):
    return jax.shard_map(
        per_device,
        mesh=mesh,
        in_specs=(P("chan", "tm"), P("chan", None), P(None, "chan", None), P()),
        out_specs=P(None, "chan", "tm"),
        check_vma=False,
    )
```
